32 devices in a mesh: ka: 16 (over z, y, x), orb: 2 (over core).
Axes of the slice: x: 2, y: 2, z: 4, core: 2. Of those that a mesh axis runs over, the one named last changes fastest.
Arguments:
- coefficients: bfloat16 [16, 8192, 128], P('ka', 'orb'), may hold values from -0.59765625 to 0.59765625
- potential: bfloat16 [3, 64, 3, 128, 128], P(None, 'orb'), may hold values from -0.3125 to 0.3125
- block_cols: int32 [3, 64, 3], P(None, 'orb'), may hold values from 0 to 63
- block_counts: int32 [3, 64], P(None, 'orb'), may hold values from 1 to 3, as said below
- partners: int32 [3, 16], replicated, may hold values from 0 to 15, each once within a row
- gaps: float32 [3, 16, 128, 128], P(None, 'ka', 'orb'), may hold values from 0.5 to 4
Outputs:
- couplings: float32 [3, 16, 128, 128], P(None, 'ka', 'orb')
The draws below stay inside these ranges and needn't reach their ends.
Inputs may be any that keep to these rules, and one draw needn't show every extreme that they name: `partners`: each row names every k-point once. `block_cols`: slots at or past a block row's count are unused and may hold any column. `block_counts`: some block row of every mode uses all 3 slots.
All inputs are finite; a program needn't handle non-finite values.
Results may differ from the reference program's by a relative error of at most 0.0029.
Values may be sent and summed in bfloat16 or wider, within the bound.
No kernel may reach another device: no remote copies, remote signals or barrier semaphores. Data moves between devices by JAX's collectives and lax.ppermute only.
A program may use at most 128 MiB of HBM per device.

```python
import math
import jax
import jax.numpy as jnp
from jax import lax

NORB = 8192
NB = 128
BS = 128
MAXB = 3
MODES = 3
NK = 16
NBR = 64


def draw_block_counts(key, part):
    counts = jax.random.randint(key, (MODES, NORB // BS), 1, MAXB + 1)
    return counts.at[:, 0].set(MAXB).astype(jnp.int32)


def with_ends(values, key, smallest, top_value):
    longest = values.shape.index(max(values.shape))
    spots = []
    for shift in (0, 1):
        where = [jax.random.randint(jax.random.fold_in(key, axis), (), 0, length) for axis, length in enumerate(values.shape)]
        where[longest] = (where[longest] + shift) % values.shape[longest]
        spots.append(tuple(where))
    return values.at[spots[0]].set(smallest).at[spots[1]].set(top_value)


def block_levels(stream_key, extent, cuts, low, top_value):
    factor_of = 1.0
    for dim, blocks in cuts:
        draws = jax.random.uniform(jax.random.fold_in(jax.random.fold_in(stream_key, 6), dim), (blocks,), jnp.float32, low / len(cuts), top_value / len(cuts))
        factor_of = factor_of * jnp.repeat(jnp.exp(draws), extent[dim] // blocks).reshape((-1,) + (1,) * (len(extent) - 1 - dim))
    return factor_of


def scatter_about(key, dims, spread, most, pieces=(), held_as=jnp.bfloat16):
    level = block_levels(key, dims, pieces, -0.22, 0.18) if pieces else 1.0
    entries = jax.random.normal(key, dims, jnp.float32) * spread * level
    return jnp.minimum(jnp.maximum(entries, -most), most).astype(held_as)


def setup_inputs(seed: int = 0) -> dict:
    arg_keys = jax.random.split(jax.random.key(seed), 7)
    return {
        "coefficients": scatter_about(arg_keys[0], (NK, NORB, NB), 0.1, 0.59765625, ((0, 16), (1, 2))),
        "potential": scatter_about(arg_keys[1], (MODES, NBR, MAXB, BS, BS), (BS * MAXB) ** -0.5, 0.3125, ((1, 2),)),
        "block_cols": with_ends(jax.random.randint(arg_keys[2], (MODES, NBR, MAXB), 0, NBR), jax.random.fold_in(arg_keys[2], 1), 0, NBR - 1).astype(jnp.int32),
        "block_counts": draw_block_counts(jax.random.fold_in(arg_keys[6], 71), 0),
        "partners": jax.vmap(lambda own: jax.random.permutation(own, NK))(jax.random.split(arg_keys[4], MODES)).reshape((MODES, NK)).astype(jnp.int32),
        "gaps": jnp.clip(jnp.exp(math.log(4.0) - 2.0794415 * jax.random.uniform(arg_keys[5], (MODES, NK, NB, NB), jnp.float32) ** block_levels(arg_keys[5], (MODES, NK, NB, NB), ((1, 16), (2, 2)), -0.2, 0.2)), 0.5, 4.0),
    }


def reference(coefficients, potential, block_cols, block_counts, partners, gaps):
    slot_index = jnp.arange(MAXB, dtype=jnp.int32)
    used = slot_index[None, None, :] < block_counts[:, :, None]
    masked = jnp.where(used[:, :, :, None, None], potential, jnp.zeros((), potential.dtype)).astype(jnp.float32)
    offsets = jnp.arange(BS, dtype=jnp.int32)
    row_index = (block_cols[:, :, :, None] * BS + offsets).reshape(MODES, -1).astype(jnp.int32)

    def one_point(point):
        current = lax.dynamic_index_in_dim(coefficients, point, 0, keepdims=False)
        results = []
        for phonon in range(MODES):
            picked = jnp.take(current, row_index[phonon], axis=0).astype(jnp.float32)
            picked = picked.reshape(NBR, MAXB, BS, NB)
            projected = jnp.einsum("rjab,rjbn->ran", masked[phonon], picked).reshape(NORB, NB).astype(jnp.bfloat16)
            matched = lax.dynamic_index_in_dim(coefficients, partners[phonon, point], 0, keepdims=False)
            raw = jnp.dot(matched.T, projected, preferred_element_type=jnp.float32)
            denominator = lax.dynamic_index_in_dim(gaps[phonon], point, 0, keepdims=False)
            results.append(raw / denominator)
        return jnp.stack(results)

    stacked = lax.map(one_point, jnp.arange(NK, dtype=jnp.int32))
    return jnp.transpose(stacked, (1, 0, 2, 3))
```

```python
import functools

import jax
import jax.numpy as jnp
from jax import lax
from jax.experimental import pallas as pl
from jax.experimental.pallas import tpu as pltpu
from jax.sharding import PartitionSpec as P

VMEM_LIMIT = 48 * 2**20
SMEM = pl.BlockSpec(memory_space=pltpu.SMEM)
VMEM = pl.BlockSpec(memory_space=pltpu.VMEM)
ANY = pl.BlockSpec(memory_space=pl.ANY)


def group_size(points, blocks):
    size = 1
    while (
        points % (2 * size) == 0 and 4 * size * size <= points and blocks % (2 * size) == 0
    ):
        size *= 2
    return size


def project_kernel(group, halves, pos, cols, counts, potential, *refs):
    sources = refs[: group * halves]
    out, whole, blocks, sems = refs[group * halves :]
    modes, rows, slots, size, _ = blocks.shape
    local_rows = potential.shape[1]
    chunk, half = pos[1], pos[2]
    copies = [
        pltpu.make_async_copy(
            potential.at[:, pl.ds(chunk * rows, rows)], blocks, sems.at[group * halves]
        )
    ]
    for shift in range(halves):
        for point in range(group):
            i = shift * group + point
            place = lax.rem(half + halves - shift, halves)
            copies.append(
                pltpu.make_async_copy(sources[i], whole.at[point, place], sems.at[i])
            )
    for copy in copies:
        copy.start()
    for copy in copies:
        copy.wait()
    for mode in range(modes):
        for row in range(rows):
            at = mode * local_rows + chunk * rows + row
            used = counts[at]
            left = []
            right = []
            for slot in range(slots):
                block = blocks[mode, row, slot]
                left.append(jnp.where(slot < used, block, jnp.zeros_like(block)))
                col = cols[at * slots + slot]
                place = lax.div(col, local_rows)
                start = pl.multiple_of(lax.rem(col, local_rows) * size, size)
                right.append(
                    jnp.concatenate(
                        [whole[point, place, pl.ds(start, size), :] for point in range(group)],
                        axis=1,
                    )
                )
            product = jnp.dot(
                jnp.concatenate(left, axis=1),
                jnp.concatenate(right, axis=0),
                preferred_element_type=jnp.float32,
            )
            turned = product.astype(jnp.bfloat16).T
            for point in range(group):
                out[point * modes + mode, :, row * size : (row + 1) * size] = turned[
                    point * size : (point + 1) * size
                ]


def project(pos, cols, counts, potential, sources, group, halves):
    modes, local_rows, slots, size, _ = potential.shape
    bands = sources[0].shape[1]
    rows = local_rows // group
    return pl.pallas_call(
        functools.partial(project_kernel, group, halves),
        out_shape=jax.ShapeDtypeStruct((group * modes, bands, rows * size), jnp.bfloat16),
        in_specs=[SMEM, SMEM, SMEM] + [ANY] * (1 + len(sources)),
        out_specs=VMEM,
        scratch_shapes=[
            pltpu.VMEM((group, halves, local_rows * size, bands), jnp.bfloat16),
            pltpu.VMEM((modes, rows, slots, size, size), jnp.bfloat16),
            pltpu.SemaphoreType.DMA((group * halves + 1,)),
        ],
        compiler_params=pltpu.CompilerParams(vmem_limit_bytes=VMEM_LIMIT),
        cost_estimate=pl.CostEstimate(
            flops=2 * modes * rows * slots * size * size * group * bands,
            bytes_accessed=30 * 2**20,
            transcendentals=0,
        ),
        name="project",
    )(pos, cols, counts, potential, *sources)


def couple_kernel(step, last, group, points, halves, pos, partners, *refs):
    sides = 1 if step == 0 else 2
    count = sides * group
    before = None
    if step > 0:
        before, refs = refs[0], refs[1:]
    projected, parts, refs = refs[0], refs[1 : 1 + count], refs[1 + count :]
    out, held, total, sems = refs
    pairs = projected.shape[0]
    modes = pairs // group
    outer, inner, half = pos[0], pos[1], pos[2]
    copies = [
        pltpu.make_async_copy(parts[i], held.at[i], sems.at[i]) for i in range(count)
    ]
    for copy in copies:
        copy.start()
    if step == 0:
        total[...] = jnp.zeros_like(total)
    else:
        total[...] = before[...]
    for copy in copies:
        copy.wait()

    def add(pair, carry):
        mine = outer * group + (inner ^ lax.div(pair, modes))
        other = partners[lax.rem(pair, modes) * points + mine]
        plane = lax.div(other, group)
        place = lax.rem(other, group) ^ inner
        if step == 0:
            hit = plane == outer
            at = place
        else:
            low = plane == outer - step
            hit = jnp.logical_or(low, plane == outer + step)
            at = place + jnp.where(low, 0, group)

        @pl.when(hit)
        def _():
            total[pair] += jnp.dot(
                projected[pair], held[at], preferred_element_type=jnp.float32
            )

        return carry

    lax.fori_loop(0, pairs, add, 0)
    if last:
        bands = total.shape[1]
        share = bands // halves
        for pair in range(pairs):
            turned = total[pair].T
            for part in range(halves):
                out[lax.rem(part + halves - half, halves), pair] = turned[
                    part * share : (part + 1) * share
                ]
    else:
        out[...] = total[...]


def couple(step, last, pos, partners, before, projected, parts, group, points, halves):
    pairs, bands, rows = projected.shape
    shape = (halves, pairs, bands // halves, bands) if last else (pairs, bands, bands)
    earlier = [] if before is None else [before]
    return pl.pallas_call(
        functools.partial(couple_kernel, step, last, group, points, halves),
        out_shape=jax.ShapeDtypeStruct(shape, jnp.float32),
        in_specs=[SMEM, SMEM] + [VMEM] * len(earlier) + [VMEM] + [ANY] * len(parts),
        out_specs=VMEM,
        scratch_shapes=[
            pltpu.VMEM((len(parts), rows, bands), jnp.bfloat16),
            pltpu.VMEM((pairs, bands, bands), jnp.float32),
            pltpu.SemaphoreType.DMA((len(parts),)),
        ],
        compiler_params=pltpu.CompilerParams(vmem_limit_bytes=VMEM_LIMIT),
        cost_estimate=pl.CostEstimate(
            flops=2 * pairs * bands * bands * rows,
            bytes_accessed=8 * 2**20,
            transcendentals=0,
        ),
        name=f"couple{step}",
    )(pos, partners, *earlier, projected, *parts)


def solution(mesh):
    points = mesh.shape["ka"]
    halves = mesh.shape["orb"]

    def per_device(coefficients, potential, block_cols, block_counts, partners, gaps):
        modes, local_rows, slots, size, _ = potential.shape
        group = group_size(points, local_rows)
        planes = points // group
        own = coefficients[0]
        rows = own.shape[0] // group
        place = lax.axis_index("ka")
        outer, inner = place // group, place % group
        half = lax.axis_index("orb")
        pos = jnp.stack([outer, inner, half]).astype(jnp.int32)
        cols = block_cols.reshape(-1)
        counts = block_counts.reshape(-1)
        pairing = partners.reshape(-1)

        def swap(value, bit):
            if bit == 0:
                return value
            return lax.ppermute(value, "ka", [(i, i ^ bit) for i in range(points)])

        def rotate(value, shift):
            if shift == 0:
                return value
            return lax.ppermute(
                value, "orb", [(i, (i + shift) % halves) for i in range(halves)]
            )

        def chunk_for(bit):
            return lax.dynamic_slice_in_dim(own, (inner ^ bit) * rows, rows, 0)

        chunks = [swap(chunk_for(bit), bit) for bit in range(group)]
        near = [swap(own, bit) for bit in range(group)]
        sources = list(near)
        for shift in range(1, halves):
            sources += [rotate(item, shift) for item in near]
        steps = [chunks]
        low, high = chunks, chunks
        for _ in range(1, planes):
            up = [(i, i + group) for i in range(points - group)]
            down = [(i + group, i) for i in range(points - group)]
            low = [lax.ppermute(item, "ka", up) for item in low]
            high = [lax.ppermute(item, "ka", down) for item in high]
            steps.append(low + high)
        projected = project(pos, cols, counts, potential, sources, group, halves)
        total = None
        for step, parts in enumerate(steps):
            total = couple(
                step,
                step == planes - 1,
                pos,
                pairing,
                total,
                projected,
                parts,
                group,
                points,
                halves,
            )
        summed = total[0]
        for shift in range(1, halves):
            summed = summed + rotate(total[shift], shift)
        summed = summed.reshape((group, modes) + summed.shape[1:])
        result = summed[0]
        for bit in range(1, group):
            result = result + swap(summed[bit], bit)
        return result[:, None] / gaps

    return jax.shard_map(
        per_device,
        mesh=mesh,
        in_specs=(
            P("ka", "orb", None),
            P(None, "orb", None, None, None),
            P(None, "orb", None),
            P(None, "orb"),
            P(),
            P(None, "ka", "orb", None),
        ),
        out_specs=P(None, "ka", "orb", None),
        check_vma=False,
    )
```

```python
import functools

import jax
import jax.numpy as jnp
from jax import lax
from jax.experimental import pallas as pl
from jax.experimental.pallas import tpu as pltpu
from jax.sharding import PartitionSpec as P

VMEM_LIMIT = 48 * 2**20
SMEM = pl.BlockSpec(memory_space=pltpu.SMEM)
VMEM = pl.BlockSpec(memory_space=pltpu.VMEM)
ANY = pl.BlockSpec(memory_space=pl.ANY)


def split_bits(points, blocks):
    bits = points.bit_length() - 1
    inside = [bit for bit in range(bits) if bit % 2 == 0][: bits // 2]
    while blocks % (1 << len(inside)):
        inside.pop()
    return inside, [bit for bit in range(bits) if bit not in inside]


def spread(value, bits):
    return sum(((value >> i) & 1) << bit for i, bit in enumerate(bits))


def gathered(value, bits):
    return sum((((value >> bit) & 1) << i for i, bit in enumerate(bits)), 0 * value)


def project_kernel(inside, halves, pos, cols, counts, potential, *refs):
    group = 1 << len(inside)
    sources = refs[: group * halves]
    out, blocks, sem = refs[group * halves :]
    modes, rows, slots, size, _ = blocks.shape
    local_rows = potential.shape[1]
    chunk, half = gathered(pos[0], inside), pos[1]
    copy = pltpu.make_async_copy(potential.at[:, pl.ds(chunk * rows, rows)], blocks, sem)
    copy.start()
    copy.wait()
    for mode in range(modes):
        for row in range(rows):
            at = mode * local_rows + chunk * rows + row
            used = counts[at]
            left = []
            right = []
            for slot in range(slots):
                block = blocks[mode, row, slot]
                left.append(jnp.where(slot < used, block, jnp.zeros_like(block)))
                col = cols[at * slots + slot]
                shift = lax.rem(half + halves - lax.div(col, local_rows), halves)
                start = pl.multiple_of(lax.rem(col, local_rows) * size, size)
                chosen = []
                for point in range(group):
                    value = sources[point][pl.ds(start, size), :]
                    for other in range(1, halves):
                        value = jnp.where(
                            shift == other,
                            sources[other * group + point][pl.ds(start, size), :],
                            value,
                        )
                    chosen.append(value)
                right.append(jnp.concatenate(chosen, axis=1))
            product = jnp.dot(
                jnp.concatenate(left, axis=1),
                jnp.concatenate(right, axis=0),
                preferred_element_type=jnp.float32,
            )
            turned = product.astype(jnp.bfloat16).T
            for point in range(group):
                out[point * modes + mode, :, row * size : (row + 1) * size] = turned[
                    point * size : (point + 1) * size
                ]


def project(pos, cols, counts, potential, sources, inside, halves):
    group = 1 << len(inside)
    modes, local_rows, slots, size, _ = potential.shape
    bands = sources[0].shape[1]
    rows = local_rows // group
    return pl.pallas_call(
        functools.partial(project_kernel, inside, halves),
        out_shape=jax.ShapeDtypeStruct((group * modes, bands, rows * size), jnp.bfloat16),
        in_specs=[SMEM, SMEM, SMEM, ANY] + [VMEM] * len(sources),
        out_specs=VMEM,
        scratch_shapes=[
            pltpu.VMEM((modes, rows, slots, size, size), jnp.bfloat16),
            pltpu.SemaphoreType.DMA,
        ],
        compiler_params=pltpu.CompilerParams(vmem_limit_bytes=VMEM_LIMIT),
        cost_estimate=pl.CostEstimate(
            flops=2 * modes * rows * slots * size * size * group * bands,
            bytes_accessed=16 * 2**20,
            transcendentals=0,
        ),
        name="project",
    )(pos, cols, counts, potential, *sources)


def couple_kernel(first, last, inside, outside, halves, pos, partners, *refs):
    group = 1 << len(inside)
    points = group << len(outside)
    before = None
    if first > 0:
        before, refs = refs[0], refs[1:]
    projected, parts, (out, total) = refs[0], refs[1:-2], refs[-2:]
    pairs, _, rows = projected.shape
    modes = pairs // group
    me, half = pos[0], pos[1]
    if first == 0:
        total[...] = jnp.zeros_like(total)
    else:
        total[...] = before[...]

    def add(pair, carry):
        point = lax.div(pair, modes)
        mine = me ^ spread(point, inside)
        away = partners[lax.rem(pair, modes) * points + mine] ^ me
        at = (gathered(away, outside) - first) * group + gathered(away, inside)
        base = 0
        for part in parts:
            count = part.shape[0] // rows
            start = at - base
            base += count

            @pl.when(jnp.logical_and(start >= 0, start < count))
            def _(part=part, start=start):
                chunk = part[pl.ds(pl.multiple_of(start * rows, rows), rows), :]
                total[pair] += jnp.dot(
                    projected[pair], chunk, preferred_element_type=jnp.float32
                )

        return carry

    lax.fori_loop(0, pairs, add, 0)
    if last:
        bands = total.shape[1]
        share = bands // halves
        for pair in range(pairs):
            turned = total[pair].T
            for part in range(halves):
                out[lax.rem(part + halves - half, halves), pair] = turned[
                    part * share : (part + 1) * share
                ]
    else:
        out[...] = total[...]


def couple(first, last, pos, partners, before, projected, parts, inside, outside, halves):
    pairs, bands, rows = projected.shape
    shape = (halves, pairs, bands // halves, bands) if last else (pairs, bands, bands)
    earlier = [] if before is None else [before]
    return pl.pallas_call(
        functools.partial(couple_kernel, first, last, inside, outside, halves),
        out_shape=jax.ShapeDtypeStruct(shape, jnp.float32),
        in_specs=[SMEM, SMEM] + [VMEM] * (len(earlier) + 1 + len(parts)),
        out_specs=VMEM,
        scratch_shapes=[pltpu.VMEM((pairs, bands, bands), jnp.float32)],
        compiler_params=pltpu.CompilerParams(vmem_limit_bytes=VMEM_LIMIT),
        cost_estimate=pl.CostEstimate(
            flops=2 * pairs * bands * bands * rows,
            bytes_accessed=8 * 2**20,
            transcendentals=0,
        ),
        name=f"couple{first}",
    )(pos, partners, *earlier, projected, *parts)


def solution(mesh):
    points = mesh.shape["ka"]
    halves = mesh.shape["orb"]

    def per_device(coefficients, potential, block_cols, block_counts, partners, gaps):
        modes, local_rows, _, _, _ = potential.shape
        inside, outside = split_bits(points, local_rows)
        group = 1 << len(inside)
        own = coefficients[0]
        rows = own.shape[0] // group
        me = lax.axis_index("ka").astype(jnp.int32)
        chunk = gathered(me, inside)
        pos = jnp.stack([me, lax.axis_index("orb").astype(jnp.int32)])
        cols = block_cols.reshape(-1)
        counts = block_counts.reshape(-1)
        pairing = partners.reshape(-1)

        def swap(value, mask):
            return lax.ppermute(value, "ka", [(i, i ^ mask) for i in range(points)])

        def rotate(value, shift):
            return lax.ppermute(
                value, "orb", [(i, (i + shift) % halves) for i in range(halves)]
            )

        def chunk_for(point):
            return lax.dynamic_slice_in_dim(own, (chunk ^ point) * rows, rows, 0)

        def after(value, *others):
            return lax.optimization_barrier((value,) + others)[0]

        parts = [chunk_for(0)]
        parts += [swap(chunk_for(p), spread(p, inside)) for p in range(1, group)]
        pieces = [parts[0], parts[1], jnp.concatenate(parts[2:], axis=0)]
        whole_set = jnp.concatenate(parts, axis=0)
        top = 1 << outside[-1]
        first_far = swap(pieces[0], top)
        held = {0: [whole_set]}
        for i in reversed(range(len(outside) - 1)):
            for key, items in list(held.items()):
                held[key | (1 << i)] = [swap(item, 1 << outside[i]) for item in items]
        second_far = swap(after(pieces[1], first_far), top)
        near = {0: after(own, first_far, *parts)}
        for i in reversed(range(len(inside))):
            ready = [near[1 << i]] if (1 << i) in near else []
            for key, item in list(near.items()):
                if key:
                    item = after(item, second_far, *ready, *held.get(1, []))
                near[key | (1 << i)] = swap(item, 1 << inside[i])
                ready = [near[key | (1 << i)]]
        third_far = swap(after(pieces[2], second_far), top)
        far = {1 << (len(outside) - 1): [first_far, second_far, third_far]}
        for i in reversed(range(len(outside) - 1)):
            for key, items in list(far.items()):
                far[key | (1 << i)] = [
                    swap(after(item, *held[1 << i]), 1 << outside[i]) for item in items
                ]
        sets = {**held, **far}
        late = far[max(far)]
        near[group - 1] = after(near[group - 1], third_far, late[0], late[1])
        sources = [near[key] for key in range(group)]
        for shift in range(1, halves):
            sources += [rotate(near[key], shift) for key in range(group)]
        projected = project(pos, cols, counts, potential, sources, inside, halves)
        count = 1 << len(outside)
        early = [part for key in range(count - 1) for part in sets[key]]
        total = couple(
            0, False, pos, pairing, None, projected, early, inside, outside, halves
        )
        total = couple(
            count - 1, True, pos, pairing, total, projected, late, inside, outside, halves
        )
        summed = total[0]
        for shift in range(1, halves):
            summed = summed + rotate(total[shift], shift)
        summed = summed.reshape((group, modes) + summed.shape[1:])
        result = summed[0]
        for point in range(1, group):
            result = result + swap(summed[point], spread(point, inside))
        return result[:, None] / gaps

    return jax.shard_map(
        per_device,
        mesh=mesh,
        in_specs=(
            P("ka", "orb", None),
            P(None, "orb", None, None, None),
            P(None, "orb", None),
            P(None, "orb"),
            P(),
            P(None, "ka", "orb", None),
        ),
        out_specs=P(None, "ka", "orb", None),
        check_vma=False,
    )
```

```python
import functools

import jax
import jax.numpy as jnp
from jax import lax
from jax.experimental import pallas as pl
from jax.experimental.pallas import tpu as pltpu
from jax.sharding import PartitionSpec as P

VMEM_LIMIT = 48 * 2**20
SMEM = pl.BlockSpec(memory_space=pltpu.SMEM)
VMEM = pl.BlockSpec(memory_space=pltpu.VMEM)
ANY = pl.BlockSpec(memory_space=pl.ANY)


def split_bits(points, blocks):
    bits = points.bit_length() - 1
    inside = [bit for bit in range(bits) if bit % 2 == 0][: bits // 2]
    while blocks % (1 << len(inside)):
        inside.pop()
    return inside, [bit for bit in range(bits) if bit not in inside]


def spread(value, bits):
    return sum(((value >> i) & 1) << bit for i, bit in enumerate(bits))


def gathered(value, bits):
    return sum((((value >> bit) & 1) << i for i, bit in enumerate(bits)), 0 * value)


def project_kernel(orders, inside, halves, pos, cols, counts, potential, *refs):
    sources, (out, whole, blocks, sem, sems) = refs[:-5], refs[-5:]
    modes, rows, slots, size, _ = blocks.shape
    points, _, chunks, length, _ = whole.shape
    local_rows = potential.shape[1]
    chunk, half = gathered(pos[0], inside), pos[1]
    first = pltpu.make_async_copy(potential.at[:, pl.ds(chunk * rows, rows)], blocks, sem)
    first.start()
    copies = []
    for i, source in enumerate(sources):
        shift, (point, order) = i // len(orders), orders[i % len(orders)]
        place = lax.rem(half + halves - shift, halves)
        for j, other in enumerate(order):
            copies.append(
                pltpu.make_async_copy(
                    source.at[pl.ds(j * length, length)],
                    whole.at[point, place, j if other is None else chunk ^ other],
                    sems.at[len(copies)],
                )
            )
    for copy in copies:
        copy.start()
    first.wait()
    for copy in copies:
        copy.wait()
    for mode in range(modes):
        for row in range(rows):
            at = mode * local_rows + chunk * rows + row
            used = counts[at]
            left = []
            right = []
            for slot in range(slots):
                block = blocks[mode, row, slot]
                left.append(jnp.where(slot < used, block, jnp.zeros_like(block)))
                col = cols[at * slots + slot]
                place = lax.div(col, local_rows)
                inner = lax.rem(col, local_rows)
                start = pl.multiple_of(lax.rem(inner, rows) * size, size)
                right.append(
                    jnp.concatenate(
                        [
                            whole[point, place, lax.div(inner, rows), pl.ds(start, size), :]
                            for point in range(points)
                        ],
                        axis=1,
                    )
                )
            product = jnp.dot(
                jnp.concatenate(left, axis=1),
                jnp.concatenate(right, axis=0),
                preferred_element_type=jnp.float32,
            )
            turned = product.astype(jnp.bfloat16).T
            for point in range(points):
                out[point * modes + mode, :, row * size : (row + 1) * size] = turned[
                    point * size : (point + 1) * size
                ]


def project(name, pos, cols, counts, potential, sources, orders, inside, halves):
    group = 1 << len(inside)
    modes, local_rows, slots, size, _ = potential.shape
    bands = sources[0].shape[1]
    rows = local_rows // group
    points = 1 + max(point for point, _ in orders)
    count = halves * sum(len(order) for _, order in orders)
    return pl.pallas_call(
        functools.partial(project_kernel, orders, inside, halves),
        out_shape=jax.ShapeDtypeStruct((points * modes, bands, rows * size), jnp.bfloat16),
        in_specs=[SMEM, SMEM, SMEM] + [ANY] * (1 + len(sources)),
        out_specs=VMEM,
        scratch_shapes=[
            pltpu.VMEM((points, halves, group, rows * size, bands), jnp.bfloat16),
            pltpu.VMEM((modes, rows, slots, size, size), jnp.bfloat16),
            pltpu.SemaphoreType.DMA,
            pltpu.SemaphoreType.DMA((count,)),
        ],
        compiler_params=pltpu.CompilerParams(vmem_limit_bytes=VMEM_LIMIT),
        cost_estimate=pl.CostEstimate(flops=0, bytes_accessed=0, transcendentals=0),
        name=name,
    )(pos, cols, counts, potential, *sources)


def couple_kernel(jobs, last, inside, outside, halves, pos, partners, *refs):
    group = 1 << len(inside)
    points = group << len(outside)
    refs, (out, total) = refs[:-2], refs[-2:]
    me, half = pos[0], pos[1]
    for start, pairs, first, count, resumed in jobs:
        projected, refs = refs[0], refs[1:]
        parts, refs = refs[:count], refs[count:]
        rows = projected.shape[2]
        modes = total.shape[0] // group
        if resumed:
            total[start : start + pairs] = refs[0][...]
            refs = refs[1:]
        else:
            total[start : start + pairs] = jnp.zeros((pairs,) + total.shape[1:], jnp.float32)

        def add(pair, carry, start=start, first=first, parts=parts, projected=projected):
            point = lax.div(pair + start, modes)
            mine = me ^ spread(point, inside)
            away = partners[lax.rem(pair, modes) * points + mine] ^ me
            at = (gathered(away, outside) - first) * group + gathered(away, inside)
            base = 0
            for part in parts:
                held = part.shape[0] // rows
                here = at - base
                base += held

                @pl.when(jnp.logical_and(here >= 0, here < held))
                def _(part=part, here=here):
                    chunk = part[pl.ds(pl.multiple_of(here * rows, rows), rows), :]
                    total[pair + start] += jnp.dot(
                        projected[pair], chunk, preferred_element_type=jnp.float32
                    )

            return carry

        lax.fori_loop(0, pairs, add, 0)
    if last:
        bands = total.shape[1]
        share = bands // halves
        for pair in range(total.shape[0]):
            turned = total[pair].T
            for part in range(halves):
                out[lax.rem(part + halves - half, halves), pair] = turned[
                    part * share : (part + 1) * share
                ]
    else:
        out[...] = total[: out.shape[0]]


def couple(name, last, pos, partners, work, group, inside, outside, halves):
    jobs = []
    values = []
    start = 0
    for projected, first, parts, before in work:
        pairs, bands, rows = projected.shape
        jobs.append((start, pairs, first, len(parts), before is not None))
        values += [projected] + parts + ([] if before is None else [before])
        start += pairs
    total = start if last else (start // (group - 1)) * group if group > 1 else start
    shape = (halves, start, bands // halves, bands) if last else (start, bands, bands)
    return pl.pallas_call(
        functools.partial(couple_kernel, jobs, last, inside, outside, halves),
        out_shape=jax.ShapeDtypeStruct(shape, jnp.float32),
        in_specs=[SMEM, SMEM] + [VMEM] * len(values),
        out_specs=VMEM,
        scratch_shapes=[pltpu.VMEM((total, bands, bands), jnp.float32)],
        compiler_params=pltpu.CompilerParams(vmem_limit_bytes=VMEM_LIMIT),
        cost_estimate=pl.CostEstimate(flops=0, bytes_accessed=0, transcendentals=0),
        name=name,
    )(pos, partners, *values)


def solution(mesh):
    points = mesh.shape["ka"]
    halves = mesh.shape["orb"]

    def per_device(coefficients, potential, block_cols, block_counts, partners, gaps):
        modes, local_rows, _, _, _ = potential.shape
        inside, outside = split_bits(points, local_rows)
        group = 1 << len(inside)
        own = coefficients[0]
        rows = own.shape[0] // group
        me = lax.axis_index("ka").astype(jnp.int32)
        chunk = gathered(me, inside)
        pos = jnp.stack([me, lax.axis_index("orb").astype(jnp.int32)])
        cols = block_cols.reshape(-1)
        counts = block_counts.reshape(-1)
        pairing = partners.reshape(-1)

        def swap(value, mask):
            return lax.ppermute(value, "ka", [(i, i ^ mask) for i in range(points)])

        def rotate(value, shift):
            return lax.ppermute(
                value, "orb", [(i, (i + shift) % halves) for i in range(halves)]
            )

        def chunk_for(point):
            return lax.dynamic_slice_in_dim(own, (chunk ^ point) * rows, rows, 0)

        def after(value, *others):
            return lax.optimization_barrier((value,) + others)[0]

        parts = [chunk_for(0)]
        parts += [swap(chunk_for(p), spread(p, inside)) for p in range(1, group)]
        top = 1 << outside[-1]
        first_far = swap(parts[0], top)
        second_far = swap(parts[1], top)
        held = {0: [jnp.concatenate(parts, axis=0)]}
        for i in reversed(range(len(outside) - 1)):
            for key, items in list(held.items()):
                held[key | (1 << i)] = [swap(item, 1 << outside[i]) for item in items]
        third_far = swap(after(jnp.concatenate(parts[2:], axis=0), first_far), top)
        far = {1 << (len(outside) - 1): [first_far, second_far, third_far]}
        for i in reversed(range(len(outside) - 1)):
            for key, items in list(far.items()):
                far[key | (1 << i)] = [
                    swap(after(item, *held[1 << i]), 1 << outside[i]) for item in items
                ]
        sets = {**held, **far}
        sets[0] = parts
        late = far[max(far)]
        own_away = [rotate(after(own, parts[1]), shift) for shift in range(1, halves)]
        chunks = {0: {p: chunk_for(p) for p in range(group)}}
        near = {}
        for i in reversed(range(len(inside))):
            bit = 1 << i
            for key in list(chunks):
                order = [p for p in range(group) if p != bit]
                rest = jnp.concatenate([chunks[key][p] for p in order], axis=0)
                if key:
                    rest = after(rest, second_far, *own_away, *near.get(bit, [])[:1])
                else:
                    rest = after(rest, parts[1], first_far)
                rest = swap(rest, spread(bit, inside))
                order = [p ^ bit for p in order]
                near[key | bit] = (rest, order)
                chunks[key | bit] = {
                    p: rest[j * rows : (j + 1) * rows] for j, p in enumerate(order)
                }
                chunks[key | bit][0] = parts[key | bit]

        def all_rows(keys):
            values = []
            orders = []
            for place, key in enumerate(keys):
                if key == 0:
                    values.append(own)
                    orders.append((place, [None] * group))
                else:
                    values += [parts[key], near[key][0]]
                    orders += [(place, [0]), (place, near[key][1])]
            return values, orders

        values, orders = all_rows(range(group - 1))
        for shift in range(1, halves):
            moved = [rotate(value, shift) for value in values[1 : len(orders)]]
            values = values + [own_away[shift - 1]] + moved
        projected = project(
            "project", pos, cols, counts, potential, values, orders, inside, halves
        )
        values, orders = all_rows([group - 1])
        for shift in range(1, halves):
            values = values + [
                rotate(after(value, projected, *late[:2]), shift) for value in values[: len(orders)]
            ]
        projected_last = project(
            "project_last", pos, cols, counts, potential, values, orders, inside, halves
        )
        count = 1 << len(outside)
        early = [part for key in range(count - 1) for part in sets[key]]
        total = couple(
            "couple",
            False,
            pos,
            pairing,
            [(projected, 0, early, None)],
            group,
            inside,
            outside,
            halves,
        )
        total = couple(
            "couple_last",
            True,
            pos,
            pairing,
            [(projected, count - 1, late, total), (projected_last, 0, early + late, None)],
            group,
            inside,
            outside,
            halves,
        )
        summed = total[0]
        for shift in range(1, halves):
            summed = summed + rotate(total[shift], shift)
        summed = summed.reshape((group, modes) + summed.shape[1:])
        result = summed[0]
        for point in range(1, group):
            result = result + swap(summed[point], spread(point, inside))
        return result[:, None] / gaps

    return jax.shard_map(
        per_device,
        mesh=mesh,
        in_specs=(
            P("ka", "orb", None),
            P(None, "orb", None, None, None),
            P(None, "orb", None),
            P(None, "orb"),
            P(),
            P(None, "ka", "orb", None),
        ),
        out_specs=P(None, "ka", "orb", None),
        check_vma=False,
    )
```

```python
import functools

import jax
import jax.numpy as jnp
from jax import lax
from jax.experimental import pallas as pl
from jax.experimental.pallas import tpu as pltpu
from jax.sharding import PartitionSpec as P

VMEM_LIMIT = 48 * 2**20
SMEM = pl.BlockSpec(memory_space=pltpu.SMEM)
VMEM = pl.BlockSpec(memory_space=pltpu.VMEM)
ANY = pl.BlockSpec(memory_space=pl.ANY)


WAITS = {
    "carry 0": [],
    "carry 1": [],
    "piece 2.0": [],
    "piece 1.0": [],
    "rest 1": ["carry 0", "piece 1.0"],
    "rest 2": ["carry 0", "piece 1.0", "carry 1"],
    "part 3": ["carry 0", "piece 1.0", "carry 1"],
    "piece 2.1": ["carry 0", "piece 1.0", "carry 1"],
    "piece 1.1": ["carry 0", "piece 1.0", "carry 1"],
    "turn 1 0": ["carry 0", "piece 1.0", "carry 1", "piece 2.0"],
    "piece 2.2": ["carry 0", "piece 1.0", "carry 1", "piece 2.0", "piece 2.1", "part 3"],
    "piece 3.0": ["carry 0", "piece 1.0", "carry 1", "piece 2.0", "piece 2.1", "part 3"],
    "rest 3": ["carry 0", "piece 1.0", "carry 1", "piece 2.0", "piece 2.1", "part 3", "turn 1 0", "rest 1", "rest 2"],
    "piece 1.2": ["carry 0", "piece 1.0", "carry 1", "piece 2.0", "piece 2.1", "part 3", "turn 1 0", "rest 1", "rest 2"],
    "turn 1 1": ["carry 0", "piece 1.0", "carry 1", "piece 2.0", "piece 2.1", "part 3", "turn 1 0", "rest 1", "rest 2"],
    "turn 1 2": ["carry 0", "piece 1.0", "carry 1", "piece 2.0", "piece 2.1", "part 3", "turn 1 0", "rest 1", "rest 2"],
    "piece 3.1": ["carry 0", "piece 1.0", "carry 1", "piece 2.0", "piece 2.1", "part 3", "turn 1 0", "rest 1", "rest 2", "piece 3.0"],
    "project": ["carry 0", "piece 1.0", "carry 1", "piece 2.0", "piece 2.1", "part 3", "turn 1 0", "rest 1", "rest 2", "piece 3.0"],
    "piece 3.2": ["carry 0", "piece 1.0", "carry 1", "piece 2.0", "piece 2.1", "part 3", "turn 1 0", "rest 1", "rest 2", "piece 3.0", "piece 1.1", "piece 1.2", "piece 2.2"],
    "turn 1 3": ["carry 0", "piece 1.0", "carry 1", "piece 2.0", "piece 2.1", "part 3", "turn 1 0", "rest 1", "rest 2", "piece 3.0", "piece 1.1", "piece 1.2", "piece 2.2", "piece 3.2", "project"],
}


def split_bits(points, blocks):
    bits = points.bit_length() - 1
    inside = [bit for bit in range(bits) if bit % 2 == 0][: bits // 2]
    while blocks % (1 << len(inside)):
        inside.pop()
    return inside, [bit for bit in range(bits) if bit not in inside]


def spread(value, bits):
    return sum(((value >> i) & 1) << bit for i, bit in enumerate(bits))


def gathered(value, bits):
    return sum((((value >> bit) & 1) << i for i, bit in enumerate(bits)), 0 * value)


def project_kernel(orders, inside, halves, pos, cols, counts, potential, *refs):
    sources, (out, whole, blocks, sem, sems) = refs[:-5], refs[-5:]
    modes, rows, slots, size, _ = blocks.shape
    points, _, chunks, length, _ = whole.shape
    local_rows = potential.shape[1]
    chunk, half = gathered(pos[0], inside), pos[1]
    first = pltpu.make_async_copy(potential.at[:, pl.ds(chunk * rows, rows)], blocks, sem)
    first.start()
    copies = []
    for i, source in enumerate(sources):
        point, shift, order = orders[i]
        place = lax.rem(half + halves - shift, halves)
        for j, other in enumerate(order):
            copies.append(
                pltpu.make_async_copy(
                    source.at[pl.ds(j * length, length)],
                    whole.at[point, place, j if other is None else chunk ^ other],
                    sems.at[len(copies)],
                )
            )
    for copy in copies:
        copy.start()
    first.wait()
    for copy in copies:
        copy.wait()
    for mode in range(modes):
        for row in range(rows):
            at = mode * local_rows + chunk * rows + row
            used = counts[at]
            left = []
            right = []
            for slot in range(slots):
                block = blocks[mode, row, slot]
                left.append(jnp.where(slot < used, block, jnp.zeros_like(block)))
                col = cols[at * slots + slot]
                place = lax.div(col, local_rows)
                inner = lax.rem(col, local_rows)
                start = pl.multiple_of(lax.rem(inner, rows) * size, size)
                right.append(
                    jnp.concatenate(
                        [
                            whole[point, place, lax.div(inner, rows), pl.ds(start, size), :]
                            for point in range(points)
                        ],
                        axis=1,
                    )
                )
            product = jnp.dot(
                jnp.concatenate(left, axis=1),
                jnp.concatenate(right, axis=0),
                preferred_element_type=jnp.float32,
            )
            turned = product.astype(jnp.bfloat16).T
            for point in range(points):
                out[point * modes + mode, :, row * size : (row + 1) * size] = turned[
                    point * size : (point + 1) * size
                ]


def project(name, pos, cols, counts, potential, sources, orders, inside, halves):
    group = 1 << len(inside)
    modes, local_rows, slots, size, _ = potential.shape
    bands = sources[0].shape[1]
    rows = local_rows // group
    points = 1 + max(point for point, _, _ in orders)
    count = sum(len(order) for _, _, order in orders)
    return pl.pallas_call(
        functools.partial(project_kernel, orders, inside, halves),
        out_shape=jax.ShapeDtypeStruct((points * modes, bands, rows * size), jnp.bfloat16),
        in_specs=[SMEM, SMEM, SMEM] + [ANY] * (1 + len(sources)),
        out_specs=VMEM,
        scratch_shapes=[
            pltpu.VMEM((points, halves, group, rows * size, bands), jnp.bfloat16),
            pltpu.VMEM((modes, rows, slots, size, size), jnp.bfloat16),
            pltpu.SemaphoreType.DMA,
            pltpu.SemaphoreType.DMA((count,)),
        ],
        compiler_params=pltpu.CompilerParams(vmem_limit_bytes=VMEM_LIMIT),
        cost_estimate=pl.CostEstimate(flops=0, bytes_accessed=0, transcendentals=0),
        name=name,
    )(pos, cols, counts, potential, *sources)


def couple_kernel(jobs, last, inside, outside, halves, pos, partners, *refs):
    group = 1 << len(inside)
    points = group << len(outside)
    refs, (out, total) = refs[:-2], refs[-2:]
    me, half = pos[0], pos[1]
    for start, pairs, first, count, resumed in jobs:
        projected, refs = refs[0], refs[1:]
        parts, refs = refs[:count], refs[count:]
        rows = projected.shape[2]
        modes = total.shape[0] // group
        if resumed:
            total[start : start + pairs] = refs[0][...]
            refs = refs[1:]
        else:
            total[start : start + pairs] = jnp.zeros((pairs,) + total.shape[1:], jnp.float32)

        def add(pair, carry, start=start, first=first, parts=parts, projected=projected):
            point = lax.div(pair + start, modes)
            mine = me ^ spread(point, inside)
            away = partners[lax.rem(pair, modes) * points + mine] ^ me
            at = (gathered(away, outside) - first) * group + gathered(away, inside)
            base = 0
            for part in parts:
                held = part.shape[0] // rows
                here = at - base
                base += held

                @pl.when(jnp.logical_and(here >= 0, here < held))
                def _(part=part, here=here):
                    chunk = part[pl.ds(pl.multiple_of(here * rows, rows), rows), :]
                    total[pair + start] += jnp.dot(
                        projected[pair], chunk, preferred_element_type=jnp.float32
                    )

            return carry

        lax.fori_loop(0, pairs, add, 0)
    if last:
        bands = total.shape[1]
        share = bands // halves
        for pair in range(total.shape[0]):
            turned = total[pair].T
            for part in range(halves):
                out[lax.rem(part + halves - half, halves), pair] = turned[
                    part * share : (part + 1) * share
                ]
    else:
        out[...] = total[: out.shape[0]]


def couple(name, last, pos, partners, work, group, inside, outside, halves):
    jobs = []
    values = []
    start = 0
    for projected, first, parts, before in work:
        pairs, bands, rows = projected.shape
        jobs.append((start, pairs, first, len(parts), before is not None))
        values += [projected] + parts + ([] if before is None else [before])
        start += pairs
    total = start if last else (start // (group - 1)) * group if group > 1 else start
    shape = (halves, start, bands // halves, bands) if last else (start, bands, bands)
    return pl.pallas_call(
        functools.partial(couple_kernel, jobs, last, inside, outside, halves),
        out_shape=jax.ShapeDtypeStruct(shape, jnp.float32),
        in_specs=[SMEM, SMEM] + [VMEM] * len(values),
        out_specs=VMEM,
        scratch_shapes=[pltpu.VMEM((total, bands, bands), jnp.float32)],
        compiler_params=pltpu.CompilerParams(vmem_limit_bytes=VMEM_LIMIT),
        cost_estimate=pl.CostEstimate(flops=0, bytes_accessed=0, transcendentals=0),
        name=name,
    )(pos, partners, *values)


def solution(mesh):
    points = mesh.shape["ka"]
    halves = mesh.shape["orb"]

    def per_device(coefficients, potential, block_cols, block_counts, partners, gaps):
        modes, local_rows, _, _, _ = potential.shape
        inside, outside = split_bits(points, local_rows)
        group = 1 << len(inside)
        own = coefficients[0]
        rows = own.shape[0] // group
        me = lax.axis_index("ka").astype(jnp.int32)
        chunk = gathered(me, inside)
        pos = jnp.stack([me, lax.axis_index("orb").astype(jnp.int32)])
        cols = block_cols.reshape(-1)
        counts = block_counts.reshape(-1)
        pairing = partners.reshape(-1)

        def swap(value, mask):
            return lax.ppermute(value, "ka", [(i, i ^ mask) for i in range(points)])

        def rotate(value, shift):
            return lax.ppermute(
                value, "orb", [(i, (i + shift) % halves) for i in range(halves)]
            )

        def chunk_for(point):
            return lax.dynamic_slice_in_dim(own, (chunk ^ point) * rows, rows, 0)

        plan = {}
        done = {}

        def get(name):
            if name not in done:
                inputs, combine, move = plan[name]
                inputs = list(inputs())
                waits = [done[other] for other in WAITS.get(name, ()) if other in done]
                if waits:
                    inputs = lax.optimization_barrier((*inputs, *waits))[: len(inputs)]
                done[name] = move(combine(inputs))
            return done[name]

        far = 1 << (len(outside) - 1)
        pieces = [[0], list(range(1, group - 1)), [group - 1]]
        orders = {}

        def joined(values):
            return jnp.concatenate(values, axis=0) if values[1:] else values[0]

        def section(value, at):
            if value.shape[0] == rows:
                return value
            return value[at * rows : (at + 1) * rows]

        def part(j):
            if j == 0:
                return chunk_for(0)
            top = j.bit_length() - 1
            return section(get(f"carry {top}"), 0) if j == 1 << top else get(f"part {j}")

        def held(key, j):
            if key == 0:
                return chunk_for(j)
            if j in orders[key]:
                return section(get(f"rest {key}"), orders[key].index(j))
            return section(get(f"carry {key.bit_length() - 1}"), j) if j else part(key)

        for j in range(1, group):
            top = j.bit_length() - 1
            lower = j ^ (1 << top)
            if lower == 0:
                plan[f"carry {top}"] = (
                    lambda j=j: [chunk_for(j + k) for k in range(j)],
                    joined,
                    functools.partial(swap, mask=spread(j, inside)),
                )
            else:
                plan[f"part {j}"] = (
                    lambda top=top, lower=lower: [section(get(f"carry {top}"), lower)],
                    joined,
                    functools.partial(swap, mask=spread(lower, inside)),
                )
        for key in range(1, 2 * far):
            bit = key & -key
            before = key ^ bit
            for i, js in enumerate(pieces):
                if before:
                    source = lambda before=before, i=i: [get(f"piece {before}.{i}")]
                else:
                    source = lambda js=js: [part(j) for j in js]
                plan[f"piece {key}.{i}"] = (
                    source,
                    joined,
                    functools.partial(swap, mask=1 << outside[bit.bit_length() - 1]),
                )
        for key in sorted(range(1, group), key=lambda k: (bin(k).count("1"), k)):
            bit = key & -key
            before = key ^ bit
            known = 1 if before else bit
            send = [j for j in range(group) if j ^ bit >= known]
            orders[key] = [j ^ bit for j in send]
            plan[f"rest {key}"] = (
                lambda before=before, send=send: [held(before, j) for j in send],
                joined,
                functools.partial(swap, mask=spread(bit, inside)),
            )
        def rows_of(key):
            if key == 0:
                return [own], [[None] * group]
            top = key.bit_length() - 1
            if key == 1 << top:
                first, order = f"carry {top}", list(range(key))
            else:
                first, order = f"part {key}", [0]
            return [get(first), get(f"rest {key}")], [order, orders[key]]

        for shift in range(1, halves):
            for key in range(group):
                plan[f"turn {shift} {key}"] = (
                    lambda key=key: rows_of(key)[0],
                    joined,
                    functools.partial(rotate, shift=shift),
                )

        def projection(name, keys):
            values = []
            places = []
            for place, key in enumerate(keys):
                sources, order = rows_of(key)
                values += sources
                places += [(place, 0, js) for js in order]
                for shift in range(1, halves):
                    values.append(get(f"turn {shift} {key}"))
                    places.append((place, shift, sum(order, [])))
            return project(
                name, pos, cols, counts, potential, values, places, inside, halves
            )

        plan["project"] = (
            lambda: [projection("project", range(group - 1))],
            joined,
            lambda value: value,
        )
        for name in WAITS:
            if name in plan:
                get(name)
        projected = get("project")
        projected_last = projection("project_last", [group - 1])
        early = [part(j) for j in range(group)]
        for key in range(1, 2 * far - 1):
            early += [get(f"piece {key}.{i}") for i in range(len(pieces))]
        late = [get(f"piece {2 * far - 1}.{i}") for i in range(len(pieces))]
        total = couple(
            "couple",
            False,
            pos,
            pairing,
            [(projected, 0, early, None)],
            group,
            inside,
            outside,
            halves,
        )
        total = couple(
            "couple_last",
            True,
            pos,
            pairing,
            [(projected, 2 * far - 1, late, total), (projected_last, 0, early + late, None)],
            group,
            inside,
            outside,
            halves,
        )
        summed = total[0]
        for shift in range(1, halves):
            summed = summed + rotate(total[shift], shift)
        summed = summed.reshape((group, modes) + summed.shape[1:])
        result = summed[0]
        for point in range(1, group):
            result = result + swap(summed[point], spread(point, inside))
        return result[:, None] / gaps

    return jax.shard_map(
        per_device,
        mesh=mesh,
        in_specs=(
            P("ka", "orb", None),
            P(None, "orb", None, None, None),
            P(None, "orb", None),
            P(None, "orb"),
            P(),
            P(None, "ka", "orb", None),
        ),
        out_specs=P(None, "ka", "orb", None),
        check_vma=False,
    )
```

```python
import functools

import jax
import jax.numpy as jnp
from jax import lax
from jax.experimental import pallas as pl
from jax.experimental.pallas import tpu as pltpu
from jax.sharding import PartitionSpec as P

SPARE_VMEM = 6 * 2**20
SMEM = pl.BlockSpec(memory_space=pltpu.SMEM)
VMEM = pl.BlockSpec(memory_space=pltpu.VMEM)
ANY = pl.BlockSpec(memory_space=pl.ANY)


FIRST = ("c0", "c1", "s1.0")
SECOND = ("p3", "r1", "r2", "s2.1", "s1.1", "s3.0")
WAITS = {
    **dict.fromkeys(FIRST, ()),
    "r1": ("c0", "s1.0"),
    **dict.fromkeys(("p3", "r2", "s2.1", "s1.1"), FIRST),
    "s3.0": ("p3",),
    **dict.fromkeys(("r3", "s2.2", "s3.1", "s1.2", "t1c0", "t1c1", "t1r1", "t1r2", "t1p3"), SECOND),
    "q": (),
    "t1r3": ("q", "s2.2", "s3.1", "s1.2"),
}


def split_bits(points, blocks):
    bits = points.bit_length() - 1
    inside = [bit for bit in range(bits) if bit % 2 == 0][: bits // 2]
    while blocks % (1 << len(inside)):
        inside.pop()
    return inside, [bit for bit in range(bits) if bit not in inside]


def spread(value, bits):
    return sum(((value >> i) & 1) << bit for i, bit in enumerate(bits))


def gathered(value, bits):
    return sum((((value >> bit) & 1) << i for i, bit in enumerate(bits)), 0 * value)


def project_kernel(orders, inside, halves, pos, cols, counts, potential, *refs):
    sources, (out, whole, blocks, sem, sems) = refs[:-5], refs[-5:]
    modes, rows, slots, size, _ = blocks.shape
    points, _, chunks, length, _ = whole.shape
    local_rows = potential.shape[1]
    chunk, half = gathered(pos[0], inside), pos[1]
    first = pltpu.make_async_copy(potential.at[:, pl.ds(chunk * rows, rows)], blocks, sem)
    first.start()
    copies = []
    for i, source in enumerate(sources):
        point, shift, order = orders[i]
        place = lax.rem(half + halves - shift, halves)
        for j, other in enumerate(order):
            copies.append(
                pltpu.make_async_copy(
                    source.at[pl.ds(j * length, length)],
                    whole.at[point, place, j if other is None else chunk ^ other],
                    sems.at[len(copies)],
                )
            )
    for copy in copies:
        copy.start()
    first.wait()
    for copy in copies:
        copy.wait()
    for mode in range(modes):
        for row in range(rows):
            at = mode * local_rows + chunk * rows + row
            used = counts[at]
            left = []
            right = []
            for slot in range(slots):
                block = blocks[mode, row, slot]
                left.append(jnp.where(slot < used, block, jnp.zeros_like(block)))
                col = cols[at * slots + slot]
                place = lax.div(col, local_rows)
                inner = lax.rem(col, local_rows)
                start = pl.multiple_of(lax.rem(inner, rows) * size, size)
                right.append(
                    jnp.concatenate(
                        [
                            whole[point, place, lax.div(inner, rows), pl.ds(start, size), :]
                            for point in range(points)
                        ],
                        axis=1,
                    )
                )
            product = jnp.dot(
                jnp.concatenate(left, axis=1),
                jnp.concatenate(right, axis=0),
                preferred_element_type=jnp.float32,
            )
            turned = product.astype(jnp.bfloat16).T
            for point in range(points):
                out[point * modes + mode, :, row * size : (row + 1) * size] = turned[
                    point * size : (point + 1) * size
                ]


def project(name, pos, cols, counts, potential, sources, orders, inside, halves):
    group = 1 << len(inside)
    modes, local_rows, slots, size, _ = potential.shape
    bands = sources[0].shape[1]
    rows = local_rows // group
    points = 1 + max(point for point, _, _ in orders)
    count = sum(len(order) for _, _, order in orders)
    held = 2 * size * (points * halves * local_rows * bands + modes * rows * slots * size)
    made = 2 * points * modes * bands * rows * size
    return pl.pallas_call(
        functools.partial(project_kernel, orders, inside, halves),
        out_shape=jax.ShapeDtypeStruct((points * modes, bands, rows * size), jnp.bfloat16),
        in_specs=[SMEM, SMEM, SMEM] + [ANY] * (1 + len(sources)),
        out_specs=VMEM,
        scratch_shapes=[
            pltpu.VMEM((points, halves, group, rows * size, bands), jnp.bfloat16),
            pltpu.VMEM((modes, rows, slots, size, size), jnp.bfloat16),
            pltpu.SemaphoreType.DMA,
            pltpu.SemaphoreType.DMA((count,)),
        ],
        compiler_params=pltpu.CompilerParams(vmem_limit_bytes=held + made + SPARE_VMEM),
        cost_estimate=pl.CostEstimate(flops=0, bytes_accessed=0, transcendentals=0),
        name=name,
    )(pos, cols, counts, potential, *sources)


def couple_kernel(jobs, last, inside, outside, halves, pos, partners, *refs):
    group = 1 << len(inside)
    points = group << len(outside)
    refs, (out, total) = refs[:-2], refs[-2:]
    me, half = pos[0], pos[1]
    for start, pairs, first, count, resumed in jobs:
        projected, refs = refs[0], refs[1:]
        parts, refs = refs[:count], refs[count:]
        rows = projected.shape[2]
        modes = total.shape[0] // group
        if resumed:
            total[start : start + pairs] = refs[0][...]
            refs = refs[1:]
        else:
            total[start : start + pairs] = jnp.zeros((pairs,) + total.shape[1:], jnp.float32)

        def add(pair, carry, start=start, first=first, parts=parts, projected=projected):
            point = lax.div(pair + start, modes)
            mine = me ^ spread(point, inside)
            away = partners[lax.rem(pair, modes) * points + mine] ^ me
            at = (gathered(away, outside) - first) * group + gathered(away, inside)
            base = 0
            for part in parts:
                held = part.shape[0] // rows
                here = at - base
                base += held

                @pl.when(jnp.logical_and(here >= 0, here < held))
                def _(part=part, here=here):
                    chunk = part[pl.ds(pl.multiple_of(here * rows, rows), rows), :]
                    total[pair + start] += jnp.dot(
                        projected[pair], chunk, preferred_element_type=jnp.float32
                    )

            return carry

        lax.fori_loop(0, pairs, add, 0)
    if last:
        bands = total.shape[1]
        share = bands // halves
        for pair in range(total.shape[0]):
            turned = total[pair].T
            for part in range(halves):
                out[lax.rem(part + halves - half, halves), pair] = turned[
                    part * share : (part + 1) * share
                ]
    else:
        out[...] = total[: out.shape[0]]


def couple(name, last, pos, partners, work, group, inside, outside, halves):
    jobs = []
    values = []
    start = 0
    for projected, first, parts, before in work:
        pairs, bands, rows = projected.shape
        jobs.append((start, pairs, first, len(parts), before is not None))
        values += [projected] + parts + ([] if before is None else [before])
        start += pairs
    total = start if last else (start // (group - 1)) * group if group > 1 else start
    shape = (halves, start, bands // halves, bands) if last else (start, bands, bands)
    held = sum(value.size * value.dtype.itemsize for value in values)
    held += 4 * (total + start) * bands * bands
    return pl.pallas_call(
        functools.partial(couple_kernel, jobs, last, inside, outside, halves),
        out_shape=jax.ShapeDtypeStruct(shape, jnp.float32),
        in_specs=[SMEM, SMEM] + [VMEM] * len(values),
        out_specs=VMEM,
        scratch_shapes=[pltpu.VMEM((total, bands, bands), jnp.float32)],
        compiler_params=pltpu.CompilerParams(vmem_limit_bytes=held + SPARE_VMEM),
        cost_estimate=pl.CostEstimate(flops=0, bytes_accessed=0, transcendentals=0),
        name=name,
    )(pos, partners, *values)


def solution(mesh):
    points = mesh.shape["ka"]
    halves = mesh.shape["orb"]

    def per_device(coefficients, potential, block_cols, block_counts, partners, gaps):
        modes, local_rows, _, _, _ = potential.shape
        inside, outside = split_bits(points, local_rows)
        group = 1 << len(inside)
        own = coefficients[0]
        rows = own.shape[0] // group
        me = lax.axis_index("ka").astype(jnp.int32)
        chunk = gathered(me, inside)
        pos = jnp.stack([me, lax.axis_index("orb").astype(jnp.int32)])
        cols = block_cols.reshape(-1)
        counts = block_counts.reshape(-1)
        pairing = partners.reshape(-1)

        def swap(value, mask):
            return lax.ppermute(value, "ka", [(i, i ^ mask) for i in range(points)])

        def rotate(value, shift):
            return lax.ppermute(
                value, "orb", [(i, (i + shift) % halves) for i in range(halves)]
            )

        def chunk_for(point):
            return lax.dynamic_slice_in_dim(own, (chunk ^ point) * rows, rows, 0)

        plan = {}
        done = {}

        def get(name):
            if name not in done:
                inputs, combine, move = plan[name]
                inputs = list(inputs())
                waits = [done[other] for other in WAITS.get(name, ()) if other in done]
                if waits:
                    inputs = lax.optimization_barrier((*inputs, *waits))[: len(inputs)]
                done[name] = move(combine(inputs))
            return done[name]

        far = 1 << (len(outside) - 1)
        pieces = {0: [[0], list(range(1, group - 1)), [group - 1]], far: [[0], list(range(1, group - 1)), [group - 1]]}
        sizes = {}
        orders = {}

        def joined(values):
            return jnp.concatenate(values, axis=0) if values[1:] else values[0]

        def section(value, at):
            if value.shape[0] == rows:
                return value
            return value[at * rows : (at + 1) * rows]

        def part(j):
            if j == 0:
                return chunk_for(0)
            top = j.bit_length() - 1
            return section(get(f"c{top}"), 0) if j == 1 << top else get(f"p{j}")

        def held(key, j):
            if key == 0:
                return chunk_for(j)
            if j in orders[key]:
                return section(get(f"r{key}"), orders[key].index(j))
            return section(get(f"c{key.bit_length() - 1}"), j) if j else part(key)

        for j in range(1, group):
            top = j.bit_length() - 1
            lower = j ^ (1 << top)
            if lower == 0:
                plan[f"c{top}"] = (
                    lambda j=j: [chunk_for(j + k) for k in range(j)],
                    joined,
                    functools.partial(swap, mask=spread(j, inside)),
                )
            else:
                plan[f"p{j}"] = (
                    lambda top=top, lower=lower: [section(get(f"c{top}"), lower)],
                    joined,
                    functools.partial(swap, mask=spread(lower, inside)),
                )
        for key in range(1, 2 * far):
            bit = key & -key
            before = key ^ bit
            sizes[key] = pieces[far if key >= far else 0]
            for i, js in enumerate(sizes[key]):
                if before:
                    source = lambda before=before, i=i: [get(f"s{before}.{i}")]
                else:
                    source = lambda js=js: [part(j) for j in js]
                plan[f"s{key}.{i}"] = (
                    source,
                    joined,
                    functools.partial(swap, mask=1 << outside[bit.bit_length() - 1]),
                )
        for key in sorted(range(1, group), key=lambda k: (bin(k).count("1"), k)):
            bit = key & -key
            before = key ^ bit
            known = 1 if before else bit
            send = [j for j in range(group) if j ^ bit >= known]
            orders[key] = [j ^ bit for j in send]
            plan[f"r{key}"] = (
                lambda before=before, send=send: [held(before, j) for j in send],
                joined,
                functools.partial(swap, mask=spread(bit, inside)),
            )
        def rows_of(key):
            top = key.bit_length() - 1
            if key == 1 << top:
                return [(f"c{top}", list(range(key))), (f"r{key}", orders[key])]
            return [(f"p{key}", [0]), (f"r{key}", orders[key])]

        for shift in range(1, halves):
            turn = functools.partial(rotate, shift=shift)
            plan[f"t{shift}o"] = (lambda: [own], joined, turn)
            for key in range(1, group):
                for name, _ in rows_of(key):
                    plan[f"t{shift}{name}"] = (lambda name=name: [get(name)], joined, turn)

        def projection(name, keys):
            values = []
            places = []
            for shift in range(halves):
                away = f"t{shift}" if shift else ""
                for place, key in enumerate(keys):
                    if key == 0:
                        values.append(get(away + "o") if shift else own)
                        places.append((place, shift, [None] * group))
                        continue
                    for source, order in rows_of(key):
                        values.append(get(away + source))
                        places.append((place, shift, order))
            return project(
                name, pos, cols, counts, potential, values, places, inside, halves
            )

        plan["q"] = (
            lambda: [projection("project", range(group - 1))],
            joined,
            lambda value: value,
        )
        for name in WAITS:
            if name in plan:
                get(name)
        projected = get("q")
        projected_last = projection("project_last", [group - 1])
        early = [part(j) for j in range(group)]
        for key in range(1, 2 * far - 1):
            early += [get(f"s{key}.{i}") for i in range(len(sizes[key]))]
        late = [get(f"s{2 * far - 1}.{i}") for i in range(len(sizes[2 * far - 1]))]
        total = couple(
            "couple",
            False,
            pos,
            pairing,
            [(projected, 0, early, None)],
            group,
            inside,
            outside,
            halves,
        )
        total = couple(
            "couple_last",
            True,
            pos,
            pairing,
            [(projected, 2 * far - 1, late, total), (projected_last, 0, early + late, None)],
            group,
            inside,
            outside,
            halves,
        )
        summed = total[0]
        for shift in range(1, halves):
            summed = summed + rotate(total[shift], shift)
        summed = summed.reshape((group, modes) + summed.shape[1:])
        result = summed[0]
        for point in range(1, group):
            result = result + swap(summed[point], spread(point, inside))
        return result[:, None] / gaps

    return jax.shard_map(
        per_device,
        mesh=mesh,
        in_specs=(
            P("ka", "orb", None),
            P(None, "orb", None, None, None),
            P(None, "orb", None),
            P(None, "orb"),
            P(),
            P(None, "ka", "orb", None),
        ),
        out_specs=P(None, "ka", "orb", None),
        check_vma=False,
    )
```

```python
import functools

import jax
import jax.numpy as jnp
from jax import lax
from jax.experimental import pallas as pl
from jax.experimental.pallas import tpu as pltpu
from jax.sharding import PartitionSpec as P

SPARE_VMEM = 6 * 2**20
SMEM = pl.BlockSpec(memory_space=pltpu.SMEM)
VMEM = pl.BlockSpec(memory_space=pltpu.VMEM)
ANY = pl.BlockSpec(memory_space=pl.ANY)


FIRST = ("c0", "c1", "s1.0")
SECOND = ("p3", "r1", "r2", "s2.1", "s1.1", "s3.0")
WAITS = {
    **dict.fromkeys(FIRST, ()),
    "r1": ("c0", "s1.0"),
    **dict.fromkeys(("p3", "r2", "s2.1", "s1.1"), FIRST),
    "s3.0": ("p3",),
    **dict.fromkeys(("r3", "s2.2", "s3.1", "s1.2", "t1c0", "t1c1", "t1r1", "t1r2", "t1p3"), SECOND),
    "q": (),
    "t1r3": ("q", "s2.2", "s3.1", "s1.2"),
}


def in_hbm(value):
    return pltpu.with_memory_space_constraint(value, pltpu.HBM)


def in_vmem(value):
    return pltpu.with_memory_space_constraint(value, pltpu.VMEM)


def split_bits(points, blocks):
    bits = points.bit_length() - 1
    inside = [bit for bit in range(bits) if bit % 2 == 0][: bits // 2]
    while blocks % (1 << len(inside)):
        inside.pop()
    return inside, [bit for bit in range(bits) if bit not in inside]


def spread(value, bits):
    return sum(((value >> i) & 1) << bit for i, bit in enumerate(bits))


def gathered(value, bits):
    return sum((((value >> bit) & 1) << i for i, bit in enumerate(bits)), 0 * value)


def project_kernel(orders, inside, halves, pos, cols, counts, potential, *refs):
    sources, (out, whole, blocks, sem, sems) = refs[:-5], refs[-5:]
    modes, rows, slots, size, _ = blocks.shape
    points, _, chunks, length, _ = whole.shape
    local_rows = potential.shape[1]
    chunk, half = gathered(pos[0], inside), pos[1]
    first = pltpu.make_async_copy(potential.at[:, pl.ds(chunk * rows, rows)], blocks, sem)
    first.start()
    copies = []
    for i, source in enumerate(sources):
        point, shift, order = orders[i]
        place = lax.rem(half + halves - shift, halves)
        for j, other in enumerate(order):
            copies.append(
                pltpu.make_async_copy(
                    source.at[pl.ds(j * length, length)],
                    whole.at[point, place, j if other is None else chunk ^ other],
                    sems.at[len(copies)],
                )
            )
    for copy in copies:
        copy.start()
    first.wait()
    for copy in copies:
        copy.wait()
    for mode in range(modes):
        for row in range(rows):
            at = mode * local_rows + chunk * rows + row
            used = counts[at]
            left = []
            right = []
            for slot in range(slots):
                block = blocks[mode, row, slot]
                left.append(jnp.where(slot < used, block, jnp.zeros_like(block)))
                col = cols[at * slots + slot]
                place = lax.div(col, local_rows)
                inner = lax.rem(col, local_rows)
                start = pl.multiple_of(lax.rem(inner, rows) * size, size)
                right.append(
                    jnp.concatenate(
                        [
                            whole[point, place, lax.div(inner, rows), pl.ds(start, size), :]
                            for point in range(points)
                        ],
                        axis=1,
                    )
                )
            product = jnp.dot(
                jnp.concatenate(left, axis=1),
                jnp.concatenate(right, axis=0),
                preferred_element_type=jnp.float32,
            )
            turned = product.astype(jnp.bfloat16).T
            for point in range(points):
                out[point * modes + mode, :, row * size : (row + 1) * size] = turned[
                    point * size : (point + 1) * size
                ]


def project(name, pos, cols, counts, potential, sources, orders, inside, halves):
    group = 1 << len(inside)
    modes, local_rows, slots, size, _ = potential.shape
    bands = sources[0].shape[1]
    rows = local_rows // group
    points = 1 + max(point for point, _, _ in orders)
    count = sum(len(order) for _, _, order in orders)
    held = 2 * size * (points * halves * local_rows * bands + modes * rows * slots * size)
    made = 2 * points * modes * bands * rows * size
    return pl.pallas_call(
        functools.partial(project_kernel, orders, inside, halves),
        out_shape=jax.ShapeDtypeStruct((points * modes, bands, rows * size), jnp.bfloat16),
        in_specs=[SMEM, SMEM, SMEM] + [ANY] * (1 + len(sources)),
        out_specs=VMEM,
        scratch_shapes=[
            pltpu.VMEM((points, halves, group, rows * size, bands), jnp.bfloat16),
            pltpu.VMEM((modes, rows, slots, size, size), jnp.bfloat16),
            pltpu.SemaphoreType.DMA,
            pltpu.SemaphoreType.DMA((count,)),
        ],
        compiler_params=pltpu.CompilerParams(vmem_limit_bytes=held + made + SPARE_VMEM),
        cost_estimate=pl.CostEstimate(flops=0, bytes_accessed=0, transcendentals=0),
        name=name,
    )(pos, cols, counts, in_hbm(potential), *[in_vmem(x) for x in sources])


def couple_kernel(jobs, last, inside, outside, halves, pos, partners, *refs):
    group = 1 << len(inside)
    points = group << len(outside)
    refs, (out, total) = refs[:-2], refs[-2:]
    me, half = pos[0], pos[1]
    for start, pairs, first, count, resumed in jobs:
        projected, refs = refs[0], refs[1:]
        parts, refs = refs[:count], refs[count:]
        rows = projected.shape[2]
        modes = total.shape[0] // group
        if resumed:
            total[start : start + pairs] = refs[0][...]
            refs = refs[1:]
        else:
            total[start : start + pairs] = jnp.zeros((pairs,) + total.shape[1:], jnp.float32)

        def add(pair, carry, start=start, first=first, parts=parts, projected=projected):
            point = lax.div(pair + start, modes)
            mine = me ^ spread(point, inside)
            away = partners[lax.rem(pair, modes) * points + mine] ^ me
            at = (gathered(away, outside) - first) * group + gathered(away, inside)
            base = 0
            for part in parts:
                held = part.shape[0] // rows
                here = at - base
                base += held

                @pl.when(jnp.logical_and(here >= 0, here < held))
                def _(part=part, here=here):
                    chunk = part[pl.ds(pl.multiple_of(here * rows, rows), rows), :]
                    total[pair + start] += jnp.dot(
                        projected[pair], chunk, preferred_element_type=jnp.float32
                    )

            return carry

        lax.fori_loop(0, pairs, add, 0)
    if last:
        bands = total.shape[1]
        share = bands // halves
        for pair in range(total.shape[0]):
            turned = total[pair].T
            for part in range(halves):
                out[lax.rem(part + halves - half, halves), pair] = turned[
                    part * share : (part + 1) * share
                ]
    else:
        out[...] = total[: out.shape[0]]


def couple(name, last, pos, partners, work, group, inside, outside, halves):
    jobs = []
    values = []
    start = 0
    for projected, first, parts, before in work:
        pairs, bands, rows = projected.shape
        jobs.append((start, pairs, first, len(parts), before is not None))
        values += [projected] + parts + ([] if before is None else [before])
        start += pairs
    total = start if last else (start // (group - 1)) * group if group > 1 else start
    shape = (halves, start, bands // halves, bands) if last else (start, bands, bands)
    held = sum(value.size * value.dtype.itemsize for value in values)
    held += 4 * (total + start) * bands * bands
    return pl.pallas_call(
        functools.partial(couple_kernel, jobs, last, inside, outside, halves),
        out_shape=jax.ShapeDtypeStruct(shape, jnp.float32),
        in_specs=[SMEM, SMEM] + [VMEM] * len(values),
        out_specs=VMEM,
        scratch_shapes=[pltpu.VMEM((total, bands, bands), jnp.float32)],
        compiler_params=pltpu.CompilerParams(vmem_limit_bytes=held + SPARE_VMEM),
        cost_estimate=pl.CostEstimate(flops=0, bytes_accessed=0, transcendentals=0),
        name=name,
    )(pos, partners, *[in_vmem(x) for x in values])


def solution(mesh):
    points = mesh.shape["ka"]
    halves = mesh.shape["orb"]

    def per_device(coefficients, potential, block_cols, block_counts, partners, gaps):
        modes, local_rows, _, _, _ = potential.shape
        inside, outside = split_bits(points, local_rows)
        group = 1 << len(inside)
        own = coefficients[0]
        rows = own.shape[0] // group
        me = lax.axis_index("ka").astype(jnp.int32)
        chunk = gathered(me, inside)
        pos = jnp.stack([me, lax.axis_index("orb").astype(jnp.int32)])
        cols = block_cols.reshape(-1)
        counts = block_counts.reshape(-1)
        pairing = partners.reshape(-1)

        def swap(value, mask):
            return lax.ppermute(value, "ka", [(i, i ^ mask) for i in range(points)])

        def rotate(value, shift):
            return lax.ppermute(
                value, "orb", [(i, (i + shift) % halves) for i in range(halves)]
            )

        def chunk_for(point):
            return lax.dynamic_slice_in_dim(own, (chunk ^ point) * rows, rows, 0)

        plan = {}
        done = {}

        def get(name):
            if name not in done:
                inputs, combine, move = plan[name]
                inputs = list(inputs())
                waits = [done[other] for other in WAITS.get(name, ()) if other in done]
                if waits:
                    inputs = lax.optimization_barrier((*inputs, *waits))[: len(inputs)]
                done[name] = move(combine(inputs))
            return done[name]

        far = 1 << (len(outside) - 1)
        pieces = {0: [[0], list(range(1, group - 1)), [group - 1]], far: [[0], list(range(1, group - 1)), [group - 1]]}
        sizes = {}
        orders = {}

        def joined(values):
            return jnp.concatenate(values, axis=0) if values[1:] else values[0]

        def section(value, at):
            if value.shape[0] == rows:
                return value
            return value[at * rows : (at + 1) * rows]

        def part(j):
            if j == 0:
                return chunk_for(0)
            top = j.bit_length() - 1
            return section(get(f"c{top}"), 0) if j == 1 << top else get(f"p{j}")

        def held(key, j):
            if key == 0:
                return chunk_for(j)
            if j in orders[key]:
                return section(get(f"r{key}"), orders[key].index(j))
            return section(get(f"c{key.bit_length() - 1}"), j) if j else part(key)

        for j in range(1, group):
            top = j.bit_length() - 1
            lower = j ^ (1 << top)
            if lower == 0:
                plan[f"c{top}"] = (
                    lambda j=j: [chunk_for(j + k) for k in range(j)],
                    joined,
                    functools.partial(swap, mask=spread(j, inside)),
                )
            else:
                plan[f"p{j}"] = (
                    lambda top=top, lower=lower: [section(get(f"c{top}"), lower)],
                    joined,
                    functools.partial(swap, mask=spread(lower, inside)),
                )
        for key in range(1, 2 * far):
            bit = key & -key
            before = key ^ bit
            sizes[key] = pieces[far if key >= far else 0]
            for i, js in enumerate(sizes[key]):
                if before:
                    source = lambda before=before, i=i: [get(f"s{before}.{i}")]
                else:
                    source = lambda js=js: [part(j) for j in js]
                plan[f"s{key}.{i}"] = (
                    source,
                    joined,
                    functools.partial(swap, mask=1 << outside[bit.bit_length() - 1]),
                )
        for key in sorted(range(1, group), key=lambda k: (bin(k).count("1"), k)):
            bit = key & -key
            before = key ^ bit
            known = 1 if before else bit
            send = [j for j in range(group) if j ^ bit >= known]
            orders[key] = [j ^ bit for j in send]
            plan[f"r{key}"] = (
                lambda before=before, send=send: [held(before, j) for j in send],
                joined,
                functools.partial(swap, mask=spread(bit, inside)),
            )
        def rows_of(key):
            top = key.bit_length() - 1
            if key == 1 << top:
                return [(f"c{top}", list(range(key))), (f"r{key}", orders[key])]
            return [(f"p{key}", [0]), (f"r{key}", orders[key])]

        for shift in range(1, halves):
            turn = functools.partial(rotate, shift=shift)
            plan[f"t{shift}o"] = (lambda: [own], joined, turn)
            for key in range(1, group):
                for name, _ in rows_of(key):
                    plan[f"t{shift}{name}"] = (lambda name=name: [get(name)], joined, turn)

        def projection(name, keys):
            values = []
            places = []
            for shift in range(halves):
                away = f"t{shift}" if shift else ""
                for place, key in enumerate(keys):
                    if key == 0:
                        values.append(get(away + "o") if shift else own)
                        places.append((place, shift, [None] * group))
                        continue
                    for source, order in rows_of(key):
                        values.append(get(away + source))
                        places.append((place, shift, order))
            return project(
                name, pos, cols, counts, potential, values, places, inside, halves
            )

        plan["q"] = (
            lambda: [projection("project", range(group - 1))],
            joined,
            lambda value: value,
        )
        for name in WAITS:
            if name in plan:
                get(name)
        projected = get("q")
        projected_last = projection("project_last", [group - 1])
        early = [part(j) for j in range(group)]
        for key in range(1, 2 * far - 1):
            early += [get(f"s{key}.{i}") for i in range(len(sizes[key]))]
        late = [get(f"s{2 * far - 1}.{i}") for i in range(len(sizes[2 * far - 1]))]
        total = couple(
            "couple",
            False,
            pos,
            pairing,
            [(projected, 0, early, None)],
            group,
            inside,
            outside,
            halves,
        )
        total = couple(
            "couple_last",
            True,
            pos,
            pairing,
            [(projected, 2 * far - 1, late, total), (projected_last, 0, early + late, None)],
            group,
            inside,
            outside,
            halves,
        )
        summed = total[0]
        for shift in range(1, halves):
            summed = summed + rotate(total[shift], shift)
        summed = summed.reshape((group, modes) + summed.shape[1:])
        result = summed[0]
        sent = summed.astype(jnp.bfloat16)
        for point in range(1, group):
            result = result + swap(sent[point], spread(point, inside)).astype(jnp.float32)
        return result[:, None] / gaps

    return jax.shard_map(
        per_device,
        mesh=mesh,
        in_specs=(
            P("ka", "orb", None),
            P(None, "orb", None, None, None),
            P(None, "orb", None),
            P(None, "orb"),
            P(),
            P(None, "ka", "orb", None),
        ),
        out_specs=P(None, "ka", "orb", None),
        check_vma=False,
    )
```

```python
import functools

import jax
import jax.numpy as jnp
from jax import lax
from jax.experimental import pallas as pl
from jax.experimental.pallas import tpu as pltpu
from jax.sharding import PartitionSpec as P

SPARE_VMEM = 6 * 2**20
SMEM = pl.BlockSpec(memory_space=pltpu.SMEM)
VMEM = pl.BlockSpec(memory_space=pltpu.VMEM)
ANY = pl.BlockSpec(memory_space=pl.ANY)


FIRST = ("c0", "c1", "s1.0")
SECOND = ("p3", "r1", "r2", "s2.1", "s1.1", "s3.0")
WAITS = {
    **dict.fromkeys(FIRST, ()),
    "s2.0": (),
    "t1o": ("s2.0",),
    "r1": ("c0", "s1.0"),
    **dict.fromkeys(("p3", "r2", "s2.1", "s1.1"), FIRST),
    "s3.0": ("p3",),
    **dict.fromkeys(("r3", "s2.2", "s3.1", "s1.2", "t1c0", "t1c1", "t1r1", "t1r2", "t1p3"), SECOND),
    "q": (),
    "t1r3": ("q", "s2.2", "s3.1", "s1.2"),
}


def in_hbm(value):
    return pltpu.with_memory_space_constraint(value, pltpu.HBM)


def in_vmem(value):
    return pltpu.with_memory_space_constraint(value, pltpu.VMEM)


def split_bits(points, blocks):
    bits = points.bit_length() - 1
    inside = [bit for bit in range(bits) if bit % 2 == 0][: bits // 2]
    while blocks % (1 << len(inside)):
        inside.pop()
    return inside, [bit for bit in range(bits) if bit not in inside]


def spread(value, bits):
    return sum(((value >> i) & 1) << bit for i, bit in enumerate(bits))


def gathered(value, bits):
    return sum((((value >> bit) & 1) << i for i, bit in enumerate(bits)), 0 * value)


def stitch_kernel(inside, places, pos, *refs):
    sources, (out, sems) = refs[: len(places)], refs[len(places) :]
    rows = out.shape[0] // len(places)
    chunk = gathered(pos[0], inside)
    copies = []
    for i, (source, (at, moving)) in enumerate(zip(sources, places)):
        start = ((chunk ^ at) if moving else at) * rows
        copies.append(
            pltpu.make_async_copy(
                source.at[pl.ds(pl.multiple_of(start, rows), rows)],
                out.at[pl.ds(i * rows, rows)],
                sems.at[i],
            )
        )
    for copy in copies:
        copy.start()
    for copy in copies:
        copy.wait()


def stitch(pos, rows, sources, places, inside):
    bands = sources[0].shape[1]
    return pl.pallas_call(
        functools.partial(stitch_kernel, inside, places),
        out_shape=jax.ShapeDtypeStruct((len(places) * rows, bands), sources[0].dtype),
        in_specs=[SMEM] + [ANY] * len(sources),
        out_specs=ANY,
        scratch_shapes=[pltpu.SemaphoreType.DMA((len(places),))],
        compiler_params=pltpu.CompilerParams(vmem_limit_bytes=2**20),
        cost_estimate=pl.CostEstimate(flops=0, bytes_accessed=0, transcendentals=0),
        name="stitch",
    )(pos, *[in_hbm(x) if p[1] else in_vmem(x) for x, p in zip(sources, places)])


def project_kernel(orders, inside, halves, pos, cols, counts, potential, *refs):
    sources, (out, whole, blocks, sem, sems) = refs[:-5], refs[-5:]
    modes, rows, slots, size, _ = blocks.shape
    points, _, chunks, length, _ = whole.shape
    local_rows = potential.shape[1]
    chunk, half = gathered(pos[0], inside), pos[1]
    first = pltpu.make_async_copy(potential.at[:, pl.ds(chunk * rows, rows)], blocks, sem)
    first.start()
    copies = []
    for i, source in enumerate(sources):
        point, shift, order = orders[i]
        place = lax.rem(half + halves - shift, halves)
        for j, other in enumerate(order):
            copies.append(
                pltpu.make_async_copy(
                    source.at[pl.ds(j * length, length)],
                    whole.at[point, place, j if other is None else chunk ^ other],
                    sems.at[len(copies)],
                )
            )
    for copy in copies:
        copy.start()
    first.wait()
    for copy in copies:
        copy.wait()
    for mode in range(modes):
        for row in range(rows):
            at = mode * local_rows + chunk * rows + row
            used = counts[at]
            left = []
            right = []
            for slot in range(slots):
                block = blocks[mode, row, slot]
                left.append(jnp.where(slot < used, block, jnp.zeros_like(block)))
                col = cols[at * slots + slot]
                place = lax.div(col, local_rows)
                inner = lax.rem(col, local_rows)
                start = pl.multiple_of(lax.rem(inner, rows) * size, size)
                right.append(
                    jnp.concatenate(
                        [
                            whole[point, place, lax.div(inner, rows), pl.ds(start, size), :]
                            for point in range(points)
                        ],
                        axis=1,
                    )
                )
            product = jnp.dot(
                jnp.concatenate(left, axis=1),
                jnp.concatenate(right, axis=0),
                preferred_element_type=jnp.float32,
            )
            turned = product.astype(jnp.bfloat16).T
            for point in range(points):
                out[point * modes + mode, :, row * size : (row + 1) * size] = turned[
                    point * size : (point + 1) * size
                ]


def project(name, pos, cols, counts, potential, sources, orders, inside, halves):
    group = 1 << len(inside)
    modes, local_rows, slots, size, _ = potential.shape
    bands = sources[0].shape[1]
    rows = local_rows // group
    points = 1 + max(point for point, _, _ in orders)
    count = sum(len(order) for _, _, order in orders)
    held = 2 * size * (points * halves * local_rows * bands + modes * rows * slots * size)
    made = 2 * points * modes * bands * rows * size
    return pl.pallas_call(
        functools.partial(project_kernel, orders, inside, halves),
        out_shape=jax.ShapeDtypeStruct((points * modes, bands, rows * size), jnp.bfloat16),
        in_specs=[SMEM, SMEM, SMEM] + [ANY] * (1 + len(sources)),
        out_specs=VMEM,
        scratch_shapes=[
            pltpu.VMEM((points, halves, group, rows * size, bands), jnp.bfloat16),
            pltpu.VMEM((modes, rows, slots, size, size), jnp.bfloat16),
            pltpu.SemaphoreType.DMA,
            pltpu.SemaphoreType.DMA((count,)),
        ],
        compiler_params=pltpu.CompilerParams(vmem_limit_bytes=held + made + SPARE_VMEM),
        cost_estimate=pl.CostEstimate(flops=0, bytes_accessed=0, transcendentals=0),
        name=name,
    )(pos, cols, counts, in_hbm(potential), *sources)


def couple_kernel(jobs, last, inside, outside, halves, pos, partners, *refs):
    group = 1 << len(inside)
    points = group << len(outside)
    refs, (out, total) = refs[:-2], refs[-2:]
    me, half = pos[0], pos[1]
    for start, pairs, first, counts, resumed in jobs:
        projected, refs = refs[0], refs[1:]
        parts, refs = refs[: len(counts)], refs[len(counts) :]
        rows = projected.shape[2]
        modes = total.shape[0] // group
        if resumed:
            total[start : start + pairs] = refs[0][...]
            refs = refs[1:]
        else:
            total[start : start + pairs] = jnp.zeros((pairs,) + total.shape[1:], jnp.float32)

        def add(
            pair,
            carry,
            start=start,
            first=first,
            parts=tuple(zip(parts, counts)),
            projected=projected,
        ):
            point = lax.div(pair + start, modes)
            mine = me ^ spread(point, inside)
            away = partners[lax.rem(pair, modes) * points + mine] ^ me
            at = (gathered(away, outside) - first) * group + gathered(away, inside)
            base = 0
            for part, held in parts:
                here = at - base
                base += held

                @pl.when(jnp.logical_and(here >= 0, here < held))
                def _(part=part, here=here):
                    chunk = part[pl.ds(pl.multiple_of(here * rows, rows), rows), :]
                    total[pair + start] += jnp.dot(
                        projected[pair], chunk, preferred_element_type=jnp.float32
                    )

            return carry

        lax.fori_loop(0, pairs, add, 0)
    if last:
        bands = total.shape[1]
        share = bands // halves
        for pair in range(total.shape[0]):
            turned = total[pair].T
            for part in range(halves):
                out[lax.rem(part + halves - half, halves), pair] = turned[
                    part * share : (part + 1) * share
                ]
    else:
        out[...] = total[: out.shape[0]]


def couple(name, last, pos, partners, work, group, inside, outside, halves):
    jobs = []
    values = []
    start = 0
    for projected, first, parts, before in work:
        pairs, bands, rows = projected.shape
        jobs.append((start, pairs, first, [count for _, count in parts], before is not None))
        values += [projected] + [value for value, _ in parts]
        values += [] if before is None else [before]
        start += pairs
    total = start if last else (start // (group - 1)) * group if group > 1 else start
    shape = (halves, start, bands // halves, bands) if last else (start, bands, bands)
    held = sum(value.size * value.dtype.itemsize for value in values)
    held += 4 * (total + start) * bands * bands
    return pl.pallas_call(
        functools.partial(couple_kernel, jobs, last, inside, outside, halves),
        out_shape=jax.ShapeDtypeStruct(shape, jnp.float32),
        in_specs=[SMEM, SMEM] + [VMEM] * len(values),
        out_specs=VMEM,
        scratch_shapes=[pltpu.VMEM((total, bands, bands), jnp.float32)],
        compiler_params=pltpu.CompilerParams(vmem_limit_bytes=held + SPARE_VMEM),
        cost_estimate=pl.CostEstimate(flops=0, bytes_accessed=0, transcendentals=0),
        name=name,
    )(pos, partners, *[in_vmem(x) for x in values])


def solution(mesh):
    points = mesh.shape["ka"]
    halves = mesh.shape["orb"]

    def per_device(coefficients, potential, block_cols, block_counts, partners, gaps):
        modes, local_rows, _, _, _ = potential.shape
        inside, outside = split_bits(points, local_rows)
        group = 1 << len(inside)
        own = coefficients[0]
        rows = own.shape[0] // group
        me = lax.axis_index("ka").astype(jnp.int32)
        chunk = gathered(me, inside)
        pos = jnp.stack([me, lax.axis_index("orb").astype(jnp.int32)])
        pos, cols, counts, pairing, own = lax.optimization_barrier(
            (pos, block_cols.reshape(-1), block_counts.reshape(-1), partners.reshape(-1), own)
        )

        def swap(value, mask):
            return lax.ppermute(value, "ka", [(i, i ^ mask) for i in range(points)])

        def rotate(value, shift):
            return lax.ppermute(
                value, "orb", [(i, (i + shift) % halves) for i in range(halves)]
            )

        plan = {}
        done = {}

        def get(name):
            if name not in done:
                inputs, move = plan[name]
                inputs = [item if isinstance(item, tuple) else (item, None) for item in inputs()]
                places = [item[1:] for item in inputs]
                inputs = [item[0] for item in inputs]
                waits = [done[other] for other in WAITS.get(name, ()) if other in done]
                if waits:
                    inputs = lax.optimization_barrier((*inputs, *waits))[: len(inputs)]
                whole = places[0] == (None,)
                done[name] = move(inputs[0] if whole else joined(places, inputs))
            return done[name]

        far = 1 << (len(outside) - 1)
        pieces = {0: [[0], list(range(1, group - 1)), [group - 1]], far: [[0], list(range(1, group - 1)), [group - 1]]}
        sizes = {}
        orders = {}

        mine = lax.dynamic_slice_in_dim(own, chunk * rows, rows, 0)

        def part(j):
            if j == 0:
                return mine, 0, False
            top = j.bit_length() - 1
            return (get(f"c{top}") if j == 1 << top else get(f"p{j}")), 0, False

        def held(key, j):
            if key == 0:
                return own, j, True
            if j in orders[key]:
                return get(f"r{key}"), orders[key].index(j), False
            return (get(f"c{key.bit_length() - 1}"), j, False) if j else part(key)

        def joined(places, values):
            if len(values) == 1 and values[0].shape[0] == rows:
                return values[0]
            return stitch(pos, rows, values, places, inside)

        for j in range(1, group):
            top = j.bit_length() - 1
            lower = j ^ (1 << top)
            if lower == 0:
                plan[f"c{top}"] = (
                    lambda j=j: [held(0, j + k) for k in range(j)],
                    functools.partial(swap, mask=spread(j, inside)),
                )
            else:
                plan[f"p{j}"] = (
                    lambda top=top, lower=lower: [(get(f"c{top}"), lower, False)],
                    functools.partial(swap, mask=spread(lower, inside)),
                )
        for key in range(1, 2 * far):
            bit = key & -key
            before = key ^ bit
            sizes[key] = pieces[far if key >= far else 0]
            for i, js in enumerate(sizes[key]):
                if before:
                    source = lambda before=before, i=i: [get(f"s{before}.{i}")]
                else:
                    source = lambda js=js: [part(j) for j in js]
                plan[f"s{key}.{i}"] = (
                    source,
                    functools.partial(swap, mask=1 << outside[bit.bit_length() - 1]),
                )
        for key in sorted(range(1, group), key=lambda k: (bin(k).count("1"), k)):
            bit = key & -key
            before = key ^ bit
            known = 1 if before else bit
            send = [j for j in range(group) if j ^ bit >= known]
            orders[key] = [j ^ bit for j in send]
            plan[f"r{key}"] = (
                lambda before=before, send=send: [held(before, j) for j in send],
                functools.partial(swap, mask=spread(bit, inside)),
            )
        def rows_of(key):
            top = key.bit_length() - 1
            if key == 1 << top:
                return [(f"c{top}", list(range(key))), (f"r{key}", orders[key])]
            return [(f"p{key}", [0]), (f"r{key}", orders[key])]

        for shift in range(1, halves):
            turn = functools.partial(rotate, shift=shift)
            plan[f"t{shift}o"] = (lambda: [own], turn)
            for key in range(1, group):
                for name, _ in rows_of(key):
                    plan[f"t{shift}{name}"] = (lambda name=name: [get(name)], turn)

        def projection(name, keys):
            values = []
            places = []
            for shift in range(halves):
                away = f"t{shift}" if shift else ""
                for place, key in enumerate(keys):
                    if key == 0:
                        values.append(in_vmem(get(away + "o")) if shift else in_hbm(own))
                        places.append((place, shift, [None] * group))
                        continue
                    for source, order in rows_of(key):
                        values.append(in_vmem(get(away + source)))
                        places.append((place, shift, order))
            return project(
                name, pos, cols, counts, potential, values, places, inside, halves
            )

        plan["q"] = (
            lambda: [projection("project", range(group - 1))],
            lambda value: value,
        )
        for name in WAITS:
            if name in plan:
                get(name)
        projected = get("q")
        projected_last = projection("project_last", [group - 1])
        early = [(part(j)[0], 1) for j in range(group)]
        for key in range(1, 2 * far - 1):
            early += [(get(f"s{key}.{i}"), len(js)) for i, js in enumerate(sizes[key])]
        key = 2 * far - 1
        late = [(get(f"s{key}.{i}"), len(js)) for i, js in enumerate(sizes[key])]
        total = couple(
            "couple",
            False,
            pos,
            pairing,
            [(projected, 0, early, None)],
            group,
            inside,
            outside,
            halves,
        )
        total = couple(
            "couple_last",
            True,
            pos,
            pairing,
            [(projected, 2 * far - 1, late, total), (projected_last, 0, early + late, None)],
            group,
            inside,
            outside,
            halves,
        )
        summed = total[0]
        for shift in range(1, halves):
            summed = summed + rotate(total[shift], shift)
        summed = summed.reshape((group, modes) + summed.shape[1:])
        result = summed[0]
        sent = summed.astype(jnp.bfloat16)
        for point in range(1, group):
            result = result + swap(sent[point], spread(point, inside)).astype(jnp.float32)
        return result[:, None] / gaps

    return jax.shard_map(
        per_device,
        mesh=mesh,
        in_specs=(
            P("ka", "orb", None),
            P(None, "orb", None, None, None),
            P(None, "orb", None),
            P(None, "orb"),
            P(),
            P(None, "ka", "orb", None),
        ),
        out_specs=P(None, "ka", "orb", None),
        check_vma=False,
    )
```

```python
import functools

import jax
import jax.numpy as jnp
from jax import lax
from jax.experimental import pallas as pl
from jax.experimental.pallas import tpu as pltpu
from jax.sharding import PartitionSpec as P

SPARE_VMEM = 6 * 2**20
SMEM = pl.BlockSpec(memory_space=pltpu.SMEM)
VMEM = pl.BlockSpec(memory_space=pltpu.VMEM)
ANY = pl.BlockSpec(memory_space=pl.ANY)


FIRST = ("c0", "c1", "s1.0")
GATHER = ("p3", "r1", "r2")
SECOND = GATHER + ("s2.1", "s1.1","s3.0")
WAITS = {
    **dict.fromkeys(FIRST, ()),
    "s2.0": (),
    "t1o": ("s2.0",),
    "r1": ("c0","s1.0"),
    **dict.fromkeys(("p3", "r2", "s2.1", "s1.1"), FIRST+("i","s2.0")),
    **dict.fromkeys(("s3.0",), ("p3",)),

    "r3": GATHER+("s1.1","s3.0"),
    **dict.fromkeys(("s2.2","s3.1","s1.2"), SECOND),
    **dict.fromkeys(("t1c0","t1c1","t1r1","t1r2","t1p3"), SECOND),
    "q": (),

    "t1r3": ("q","s2.2","s3.1","s1.2"),
}


def in_hbm(value):
    return pltpu.with_memory_space_constraint(value, pltpu.HBM)


def in_vmem(value):
    return pltpu.with_memory_space_constraint(value, pltpu.VMEM)


def split_bits(points, blocks):
    bits = points.bit_length() - 1
    inside = [bit for bit in range(bits) if bit % 2 == 0][: bits // 2]
    while blocks % (1 << len(inside)):
        inside.pop()
    return inside, [bit for bit in range(bits) if bit not in inside]


def spread(value, bits):
    return sum(((value >> i) & 1) << bit for i, bit in enumerate(bits))


def gathered(value, bits):
    return sum((((value >> bit) & 1) << i for i, bit in enumerate(bits)), 0 * value)


def stitch_kernel(places, *refs):
    sources, (out, sems) = refs[: len(places)], refs[len(places) :]
    rows = out.shape[0] // len(places)
    copies = []
    for i, (source, at) in enumerate(zip(sources, places)):
        copies.append(
            pltpu.make_async_copy(
                source.at[pl.ds(at * rows, rows)],
                out.at[pl.ds(i * rows, rows)],
                sems.at[i],
            )
        )
    for copy in copies:
        copy.start()
    for copy in copies:
        copy.wait()


def stitch(rows, sources, places):
    bands = sources[0].shape[1]
    return pl.pallas_call(
        functools.partial(stitch_kernel, places),
        out_shape=jax.ShapeDtypeStruct((len(places) * rows, bands), sources[0].dtype),
        in_specs=[ANY] * len(sources),
        out_specs=ANY,
        scratch_shapes=[pltpu.SemaphoreType.DMA((len(places),))],
        compiler_params=pltpu.CompilerParams(vmem_limit_bytes=2**20),
        cost_estimate=pl.CostEstimate(flops=0, bytes_accessed=0, transcendentals=0),
        name="stitch",
    )(*[in_vmem(source) for source in sources])


def project_kernel(orders, inside, halves, pos, cols, counts, potential, *refs):
    sources, (out, whole, blocks, sem, sems) = refs[:-5], refs[-5:]
    modes, rows, slots, size, _ = blocks.shape
    points, _, chunks, length, _ = whole.shape
    local_rows = potential.shape[1]
    chunk, half = gathered(pos[0], inside), pos[1]
    first = pltpu.make_async_copy(potential.at[:, pl.ds(chunk * rows, rows)], blocks, sem)
    first.start()
    copies = []
    for i, source in enumerate(sources):
        point, shift, order = orders[i]
        place = lax.rem(half + halves - shift, halves)
        for j, other in enumerate(order):
            copies.append(
                pltpu.make_async_copy(
                    source.at[pl.ds(j * length, length)],
                    whole.at[point, place, j if other is None else chunk ^ other],
                    sems.at[len(copies)],
                )
            )
    for copy in copies:
        copy.start()
    first.wait()
    for copy in copies:
        copy.wait()
    for mode in range(modes):
        for row in range(rows):
            at = mode * local_rows + chunk * rows + row
            used = counts[at]
            left = []
            right = []
            for slot in range(slots):
                block = blocks[mode, row, slot]
                left.append(jnp.where(slot < used, block, jnp.zeros_like(block)))
                col = cols[at * slots + slot]
                place = lax.div(col, local_rows)
                inner = lax.rem(col, local_rows)
                start = pl.multiple_of(lax.rem(inner, rows) * size, size)
                right.append(
                    jnp.concatenate(
                        [
                            whole[point, place, lax.div(inner, rows), pl.ds(start, size), :]
                            for point in range(points)
                        ],
                        axis=1,
                    )
                )
            product = jnp.dot(
                jnp.concatenate(left, axis=1),
                jnp.concatenate(right, axis=0),
                preferred_element_type=jnp.float32,
            )
            turned = product.astype(jnp.bfloat16).T
            for point in range(points):
                out[point * modes + mode, :, row * size : (row + 1) * size] = turned[
                    point * size : (point + 1) * size
                ]


def project(name, pos, cols, counts, potential, sources, orders, inside, halves):
    group = 1 << len(inside)
    modes, local_rows, slots, size, _ = potential.shape
    bands = sources[0].shape[1]
    rows = local_rows // group
    points = 1 + max(point for point, _, _ in orders)
    count = sum(len(order) for _, _, order in orders)
    held = 2 * size * (points * halves * local_rows * bands + modes * rows * slots * size)
    made = 2 * points * modes * bands * rows * size
    return pl.pallas_call(
        functools.partial(project_kernel, orders, inside, halves),
        out_shape=jax.ShapeDtypeStruct((points * modes, bands, rows * size), jnp.bfloat16),
        in_specs=[SMEM, SMEM, SMEM] + [ANY] * (1 + len(sources)),
        out_specs=VMEM,
        scratch_shapes=[
            pltpu.VMEM((points, halves, group, rows * size, bands), jnp.bfloat16),
            pltpu.VMEM((modes, rows, slots, size, size), jnp.bfloat16),
            pltpu.SemaphoreType.DMA,
            pltpu.SemaphoreType.DMA((count,)),
        ],
        compiler_params=pltpu.CompilerParams(vmem_limit_bytes=held + made + SPARE_VMEM),
        cost_estimate=pl.CostEstimate(flops=0, bytes_accessed=0, transcendentals=0),
        name=name,
    )(pos, cols, counts, in_hbm(potential), *sources)


def couple_kernel(jobs, last, inside, outside, halves, pos, partners, *refs):
    group = 1 << len(inside)
    points = group << len(outside)
    refs, (out, total) = refs[:-2], refs[-2:]
    me, half = pos[0], pos[1]
    for start, pairs, first, counts, resumed in jobs:
        projected, refs = refs[0], refs[1:]
        parts, refs = refs[: len(counts)], refs[len(counts) :]
        rows = projected.shape[2]
        modes = total.shape[0] // group
        if resumed:
            total[start : start + pairs] = refs[0][...]
            refs = refs[1:]
        else:
            total[start : start + pairs] = jnp.zeros((pairs,) + total.shape[1:], jnp.float32)

        def add(
            pair,
            carry,
            start=start,
            first=first,
            parts=tuple(zip(parts, counts)),
            projected=projected,
        ):
            point = lax.div(pair + start, modes)
            mine = me ^ spread(point, inside)
            away = partners[lax.rem(pair, modes) * points + mine] ^ me
            at = (gathered(away, outside) - first) * group + gathered(away, inside)
            base = 0
            for part, held in parts:
                here = at - base
                base += held

                @pl.when(jnp.logical_and(here >= 0, here < held))
                def _(part=part, here=here):
                    chunk = part[pl.ds(pl.multiple_of(here * rows, rows), rows), :]
                    total[pair + start] += jnp.dot(
                        projected[pair], chunk, preferred_element_type=jnp.float32
                    )

            return carry

        lax.fori_loop(0, pairs, add, 0)
    if last:
        bands = total.shape[1]
        share = bands // halves
        for pair in range(total.shape[0]):
            turned = total[pair].T
            for part in range(halves):
                out[lax.rem(part + halves - half, halves), pair] = turned[
                    part * share : (part + 1) * share
                ]
    else:
        out[...] = total[: out.shape[0]]


def couple(name, last, pos, partners, work, group, inside, outside, halves):
    jobs = []
    values = []
    start = 0
    for projected, first, parts, before in work:
        pairs, bands, rows = projected.shape
        jobs.append((start, pairs, first, [count for _, count in parts], before is not None))
        values += [projected] + [value for value, _ in parts]
        values += [] if before is None else [before]
        start += pairs
    total = start if last else (start // (group - 1)) * group if group > 1 else start
    shape = (halves, start, bands // halves, bands) if last else (start, bands, bands)
    held = sum(value.size * value.dtype.itemsize for value in values)
    held += 4 * (total + start) * bands * bands
    return pl.pallas_call(
        functools.partial(couple_kernel, jobs, last, inside, outside, halves),
        out_shape=jax.ShapeDtypeStruct(shape, jnp.float32),
        in_specs=[SMEM, SMEM] + [VMEM] * len(values),
        out_specs=VMEM,
        scratch_shapes=[pltpu.VMEM((total, bands, bands), jnp.float32)],
        compiler_params=pltpu.CompilerParams(vmem_limit_bytes=held + SPARE_VMEM),
        cost_estimate=pl.CostEstimate(flops=0, bytes_accessed=0, transcendentals=0),
        name=name,
    )(pos, partners, *[in_vmem(x) for x in values])


def solution(mesh):
    points = mesh.shape["ka"]
    halves = mesh.shape["orb"]

    def per_device(coefficients, potential, block_cols, block_counts, partners, gaps):
        modes, local_rows, _, _, _ = potential.shape
        inside, outside = split_bits(points, local_rows)
        group = 1 << len(inside)
        own = coefficients[0]
        rows = own.shape[0] // group
        me = lax.axis_index("ka").astype(jnp.int32)
        chunk = gathered(me, inside)
        pos = jnp.stack([me, lax.axis_index("orb").astype(jnp.int32)])
        pos, own = lax.optimization_barrier((pos, own))

        def swap(value, mask):
            return lax.ppermute(value, "ka", [(i, i ^ mask) for i in range(points)])

        def rotate(value, shift):
            return lax.ppermute(
                value, "orb", [(i, (i + shift) % halves) for i in range(halves)]
            )

        plan = {}
        done = {}

        def get(name):
            if name not in done:
                inputs, move = plan[name]
                inputs = [item if isinstance(item, tuple) else (item, None) for item in inputs()]
                places = [item[1:] for item in inputs]
                inputs = [item[0] for item in inputs]
                waits = [done[other] for other in WAITS.get(name, ()) if other in done]
                if waits:
                    inputs, _ = lax.optimization_barrier((inputs, waits))
                whole = places[0] == (None,)
                done[name] = move(inputs[0] if whole else joined(places, inputs))
            return done[name]

        far = 1 << (len(outside) - 1)
        pieces = {0: [[0], list(range(1, group - 1)), [group - 1]], far: [[0], list(range(1, group - 1)), [group - 1]]}
        sizes = {}
        orders = {}

        slices = [
            lax.dynamic_slice_in_dim(own, (chunk ^ j) * rows, rows, 0) for j in range(group)
        ]

        def part(j):
            if j == 0:
                return slices[0], 0, False
            top = j.bit_length() - 1
            return (get(f"c{top}") if j == 1 << top else get(f"p{j}")), 0, False

        def held(key, j):
            if key == 0:
                return slices[j], 0, True
            if j in orders[key]:
                return get(f"r{key}"), orders[key].index(j), False
            return (get(f"c{key.bit_length() - 1}"), j, False) if j else part(key)

        def joined(places, values):
            if len(values) == 1 and values[0].shape[0] == rows:
                return values[0]
            if all(value.shape[0] == rows for value in values) and places[0] == (0, True):
                return jnp.concatenate(values, axis=0)
            return stitch(rows, values, [at for at, _ in places])

        for j in range(1, group):
            top = j.bit_length() - 1
            lower = j ^ (1 << top)
            if lower == 0:
                plan[f"c{top}"] = (
                    lambda j=j: [held(0, j + k) for k in range(j)],
                    functools.partial(swap, mask=spread(j, inside)),
                )
            else:
                plan[f"p{j}"] = (
                    lambda top=top, lower=lower: [(get(f"c{top}"), lower, False)],
                    functools.partial(swap, mask=spread(lower, inside)),
                )
        for key in range(1, 2 * far):
            bit = key & -key
            before = key ^ bit
            sizes[key] = pieces[far if key >= far else 0]
            for i, js in enumerate(sizes[key]):
                if before:
                    source = lambda before=before, i=i: [get(f"s{before}.{i}")]
                else:
                    source = lambda js=js: [part(j) for j in js]
                plan[f"s{key}.{i}"] = (
                    source,
                    functools.partial(swap, mask=1 << outside[bit.bit_length() - 1]),
                )
        for key in sorted(range(1, group), key=lambda k: (bin(k).count("1"), k)):
            bit = key & -key
            before = key ^ bit
            known = 1 if before else bit
            send = [j for j in range(group) if j ^ bit >= known]
            orders[key] = [j ^ bit for j in send]
            plan[f"r{key}"] = (
                lambda before=before, send=send: [held(before, j) for j in send],
                functools.partial(swap, mask=spread(bit, inside)),
            )
        def rows_of(key):
            top = key.bit_length() - 1
            if key == 1 << top:
                return [(f"c{top}", list(range(key))), (f"r{key}", orders[key])]
            return [(f"p{key}", [0]), (f"r{key}", orders[key])]

        for shift in range(1, halves):
            turn = functools.partial(rotate, shift=shift)
            plan[f"t{shift}o"] = (lambda: [own], turn)
            for key in range(1, group):
                for name, _ in rows_of(key):
                    plan[f"t{shift}{name}"] = (lambda name=name: [get(name)], turn)

        def projection(name, keys):
            values = []
            places = []
            for shift in range(halves):
                away = f"t{shift}" if shift else ""
                for place, key in enumerate(keys):
                    if key == 0:
                        values.append(in_vmem(get(away + "o")) if shift else in_hbm(own))
                        places.append((place, shift, [None] * group))
                        continue
                    for source, order in rows_of(key):
                        values.append(in_vmem(get(away + source)))
                        places.append((place, shift, order))
            return project(
                name, pos, cols, counts, potential, values, places, inside, halves
            )

        plan["q"] = (
            lambda: [projection("project", range(group - 1))],
            lambda value: value,
        )
        tables = (block_cols.reshape(-1), block_counts.reshape(-1), partners.reshape(-1))
        tables = lax.optimization_barrier((get("c0"), *tables))[1:]
        cols, counts, pairing = done["i"] = tables
        for name in WAITS:
            if name in plan:
                get(name)
        projected = get("q")
        projected_last = projection("project_last", [group - 1])
        early = [(part(j)[0], 1) for j in range(group)]
        for key in range(1, 2 * far - 1):
            early += [(get(f"s{key}.{i}"), len(js)) for i, js in enumerate(sizes[key])]
        key = 2 * far - 1
        late = [(get(f"s{key}.{i}"), len(js)) for i, js in enumerate(sizes[key])]
        total = couple(
            "couple",
            False,
            pos,
            pairing,
            [(projected, 0, early, None)],
            group,
            inside,
            outside,
            halves,
        )
        total = couple(
            "couple_last",
            True,
            pos,
            pairing,
            [(projected, 2 * far - 1, late, total), (projected_last, 0, early + late, None)],
            group,
            inside,
            outside,
            halves,
        )
        summed = total[0]
        for shift in range(1, halves):
            summed = summed + rotate(total[shift], shift)
        summed = summed.reshape((group, modes) + summed.shape[1:])
        result = summed[0]
        sent = summed.astype(jnp.bfloat16)
        for point in range(1, group):
            result = result + swap(sent[point], spread(point, inside)).astype(jnp.float32)
        return result[:, None] / gaps

    return jax.shard_map(
        per_device,
        mesh=mesh,
        in_specs=(
            P("ka", "orb", None),
            P(None, "orb", None, None, None),
            P(None, "orb", None),
            P(None, "orb"),
            P(),
            P(None, "ka", "orb", None),
        ),
        out_specs=P(None, "ka", "orb", None),
        check_vma=False,
    )
```

```python
import functools

import jax
import jax.numpy as jnp
from jax import lax
from jax.experimental import pallas as pl
from jax.experimental.pallas import tpu as pltpu
from jax.sharding import PartitionSpec as P

SPARE_VMEM = 6 * 2**20
SMEM = pl.BlockSpec(memory_space=pltpu.SMEM)
VMEM = pl.BlockSpec(memory_space=pltpu.VMEM)
ANY = pl.BlockSpec(memory_space=pl.ANY)


FIRST = ("c0", "c1", "s1.0")
SECOND = ("p3", "r1", "r2", "s2.1", "s1.1","s3.0")
WAITS = {
    **dict.fromkeys(FIRST, ()),
    "s2.0": (),
    "t1o": ("s2.0",),
    "r1": ("c0","s1.0"),
    **dict.fromkeys(("p3", "r2", "s2.1", "s1.1"), FIRST+("i",)),
    **dict.fromkeys(("s3.0",), ("p3",)),

    **dict.fromkeys(("s2.2","s3.1","s1.2","r3","u3"), SECOND),
    **dict.fromkeys(("t1k1","t1k2"), SECOND),
    "q": (),
    "t1k3": ("q","s2.2","s3.1","s1.2"),
}


def in_hbm(value):
    return pltpu.with_memory_space_constraint(value, pltpu.HBM)


def in_vmem(value):
    return pltpu.with_memory_space_constraint(value, pltpu.VMEM)


def split_bits(points, blocks):
    bits = points.bit_length() - 1
    inside = [bit for bit in range(bits) if bit % 2 == 0][: bits // 2]
    while blocks % (1 << len(inside)):
        inside.pop()
    return inside, [bit for bit in range(bits) if bit not in inside]


def spread(value, bits):
    return sum(((value >> i) & 1) << bit for i, bit in enumerate(bits))


def gathered(value, bits):
    return sum((((value >> bit) & 1) << i for i, bit in enumerate(bits)), 0 * value)


def stitch_kernel(places, *refs):
    sources, (out, sems) = refs[: len(places)], refs[len(places) :]
    rows = out.shape[0] // len(places)
    copies = []
    for i, (source, at) in enumerate(zip(sources, places)):
        copies.append(
            pltpu.make_async_copy(
                source.at[pl.ds(at * rows, rows)],
                out.at[pl.ds(i * rows, rows)],
                sems.at[i],
            )
        )
    for copy in copies:
        copy.start()
    for copy in copies:
        copy.wait()


def stitch(rows, sources, places):
    bands = sources[0].shape[1]
    return pl.pallas_call(
        functools.partial(stitch_kernel, places),
        out_shape=jax.ShapeDtypeStruct((len(places) * rows, bands), sources[0].dtype),
        in_specs=[ANY] * len(sources),
        out_specs=ANY,
        scratch_shapes=[pltpu.SemaphoreType.DMA((len(places),))],
        compiler_params=pltpu.CompilerParams(vmem_limit_bytes=2**20),
        cost_estimate=pl.CostEstimate(flops=0, bytes_accessed=0, transcendentals=0),
        name="stitch",
    )(*[in_vmem(source) for source in sources])


def project_kernel(orders, inside, halves, pos, cols, counts, potential, *refs):
    sources, (out, whole, blocks, sem, sems) = refs[:-5], refs[-5:]
    modes, rows, slots, size, _ = blocks.shape
    points, _, chunks, length, _ = whole.shape
    local_rows = potential.shape[1]
    chunk, half = gathered(pos[0], inside), pos[1]
    first = pltpu.make_async_copy(potential.at[:, pl.ds(chunk * rows, rows)], blocks, sem)
    first.start()
    copies = []
    for i, source in enumerate(sources):
        point, shift, order = orders[i]
        place = lax.rem(half + halves - shift, halves)
        for j, other in enumerate(order):
            copies.append(
                pltpu.make_async_copy(
                    source.at[pl.ds(j * length, length)],
                    whole.at[point, place, j if other is None else chunk ^ other],
                    sems.at[len(copies)],
                )
            )
    for copy in copies:
        copy.start()
    first.wait()
    for copy in copies:
        copy.wait()
    for mode in range(modes):
        for row in range(rows):
            at = mode * local_rows + chunk * rows + row
            used = counts[at]
            left = []
            right = []
            for slot in range(slots):
                block = blocks[mode, row, slot]
                left.append(jnp.where(slot < used, block, jnp.zeros_like(block)))
                col = cols[at * slots + slot]
                place = lax.div(col, local_rows)
                inner = lax.rem(col, local_rows)
                start = pl.multiple_of(lax.rem(inner, rows) * size, size)
                right.append(
                    jnp.concatenate(
                        [
                            whole[point, place, lax.div(inner, rows), pl.ds(start, size), :]
                            for point in range(points)
                        ],
                        axis=1,
                    )
                )
            product = jnp.dot(
                jnp.concatenate(left, axis=1),
                jnp.concatenate(right, axis=0),
                preferred_element_type=jnp.float32,
            )
            turned = product.astype(jnp.bfloat16).T
            for point in range(points):
                out[point * modes + mode, :, row * size : (row + 1) * size] = turned[
                    point * size : (point + 1) * size
                ]


def project(name, pos, cols, counts, potential, sources, orders, inside, halves):
    group = 1 << len(inside)
    modes, local_rows, slots, size, _ = potential.shape
    bands = sources[0].shape[1]
    rows = local_rows // group
    points = 1 + max(point for point, _, _ in orders)
    count = sum(len(order) for _, _, order in orders)
    held = 2 * size * (points * halves * local_rows * bands + modes * rows * slots * size)
    made = 2 * points * modes * bands * rows * size
    return pl.pallas_call(
        functools.partial(project_kernel, orders, inside, halves),
        out_shape=jax.ShapeDtypeStruct((points * modes, bands, rows * size), jnp.bfloat16),
        in_specs=[SMEM, SMEM, SMEM] + [ANY] * (1 + len(sources)),
        out_specs=VMEM,
        scratch_shapes=[
            pltpu.VMEM((points, halves, group, rows * size, bands), jnp.bfloat16),
            pltpu.VMEM((modes, rows, slots, size, size), jnp.bfloat16),
            pltpu.SemaphoreType.DMA,
            pltpu.SemaphoreType.DMA((count,)),
        ],
        compiler_params=pltpu.CompilerParams(vmem_limit_bytes=held + made + SPARE_VMEM),
        cost_estimate=pl.CostEstimate(flops=0, bytes_accessed=0, transcendentals=0),
        name=name,
    )(pos, cols, counts, in_hbm(potential), *sources)


def couple_kernel(jobs, last, inside, outside, halves, pos, partners, *refs):
    group = 1 << len(inside)
    points = group << len(outside)
    refs, (out, total) = refs[:-2], refs[-2:]
    me, half = pos[0], pos[1]
    for start, pairs, first, counts, resumed in jobs:
        projected, refs = refs[0], refs[1:]
        parts, refs = refs[: len(counts)], refs[len(counts) :]
        rows = projected.shape[2]
        modes = total.shape[0] // group
        if resumed:
            total[start : start + pairs] = refs[0][...]
            refs = refs[1:]
        else:
            total[start : start + pairs] = jnp.zeros((pairs,) + total.shape[1:], jnp.float32)

        def add(
            pair,
            carry,
            start=start,
            first=first,
            parts=tuple(zip(parts, counts)),
            projected=projected,
        ):
            point = lax.div(pair + start, modes)
            mine = me ^ spread(point, inside)
            away = partners[lax.rem(pair, modes) * points + mine] ^ me
            at = (gathered(away, outside) - first) * group + gathered(away, inside)
            base = 0
            for part, held in parts:
                here = at - base
                base += held

                @pl.when(jnp.logical_and(here >= 0, here < held))
                def _(part=part, here=here):
                    chunk = part[pl.ds(pl.multiple_of(here * rows, rows), rows), :]
                    total[pair + start] += jnp.dot(
                        projected[pair], chunk, preferred_element_type=jnp.float32
                    )

            return carry

        lax.fori_loop(0, pairs, add, 0)
    if last:
        bands = total.shape[1]
        share = bands // halves
        for pair in range(total.shape[0]):
            turned = total[pair].T
            for part in range(halves):
                out[lax.rem(part + halves - half, halves), pair] = turned[
                    part * share : (part + 1) * share
                ]
    else:
        out[...] = total[: out.shape[0]]


def couple(name, last, pos, partners, work, group, inside, outside, halves):
    jobs = []
    values = []
    start = 0
    for projected, first, parts, before in work:
        pairs, bands, rows = projected.shape
        jobs.append((start, pairs, first, [count for _, count in parts], before is not None))
        values += [projected] + [value for value, _ in parts]
        values += [] if before is None else [before]
        start += pairs
    total = start if last else (start // (group - 1)) * group if group > 1 else start
    shape = (halves, start, bands // halves, bands) if last else (start, bands, bands)
    held = sum(value.size * value.dtype.itemsize for value in values)
    held += 4 * (total + start) * bands * bands
    return pl.pallas_call(
        functools.partial(couple_kernel, jobs, last, inside, outside, halves),
        out_shape=jax.ShapeDtypeStruct(shape, jnp.float32),
        in_specs=[SMEM, SMEM] + [VMEM] * len(values),
        out_specs=VMEM,
        scratch_shapes=[pltpu.VMEM((total, bands, bands), jnp.float32)],
        compiler_params=pltpu.CompilerParams(vmem_limit_bytes=held + SPARE_VMEM),
        cost_estimate=pl.CostEstimate(flops=0, bytes_accessed=0, transcendentals=0),
        name=name,
    )(pos, partners, *[in_vmem(x) for x in values])


def solution(mesh):
    points = mesh.shape["ka"]
    halves = mesh.shape["orb"]

    def per_device(coefficients, potential, block_cols, block_counts, partners, gaps):
        modes, local_rows, _, _, _ = potential.shape
        inside, outside = split_bits(points, local_rows)
        group = 1 << len(inside)
        own = coefficients[0]
        rows = own.shape[0] // group
        me = lax.axis_index("ka").astype(jnp.int32)
        chunk = gathered(me, inside)
        pos = jnp.stack([me, lax.axis_index("orb").astype(jnp.int32)])
        pos, own = lax.optimization_barrier((pos, own))

        def swap(value, mask):
            return lax.ppermute(value, "ka", [(i, i ^ mask) for i in range(points)])

        def rotate(value, shift):
            return lax.ppermute(
                value, "orb", [(i, (i + shift) % halves) for i in range(halves)]
            )

        plan = {}
        done = {}

        def get(name):
            if name not in done:
                inputs, move = plan[name]
                inputs = [item if isinstance(item, tuple) else (item, None) for item in inputs()]
                places = [item[1:] for item in inputs]
                inputs = [item[0] for item in inputs]
                waits = [done[other] for other in WAITS.get(name, ()) if other in done]
                if waits:
                    inputs, _ = lax.optimization_barrier((inputs, waits))
                whole = places[0] == (None,)
                done[name] = move(inputs[0] if whole else joined(places, inputs))
            return done[name]

        far = 1 << (len(outside) - 1)
        pieces = {0: [[0], list(range(1, group - 1)), [group - 1]], far: [[0], list(range(1, group - 1)), [group - 1]]}
        sizes = {}
        orders = {}
        joins = {}

        slices = [
            lax.dynamic_slice_in_dim(own, (chunk ^ j) * rows, rows, 0) for j in range(group)
        ]

        def part(j):
            if j == 0:
                return slices[0], 0, False
            top = j.bit_length() - 1
            return (get(f"c{top}") if j == 1 << top else get(f"p{j}")), 0, False

        def held(key, j):
            if key == 0:
                return slices[j], 0, True
            for name in (f"r{key}", f"u{key}"):
                if j in orders.get(name, ()):
                    return get(name), orders[name].index(j), False
            return (get(f"c{key.bit_length() - 1}"), j, False) if j else part(key)

        def joined(places, values):
            if len(values) == 1 and values[0].shape[0] == rows:
                return values[0]
            if all(value.shape[0] == rows for value in values) and places[0] == (0, True):
                return jnp.concatenate(values, axis=0)
            return stitch(rows, values, [at for at, _ in places])

        for j in range(1, group):
            top = j.bit_length() - 1
            lower = j ^ (1 << top)
            if lower == 0:
                plan[f"c{top}"] = (
                    lambda j=j: [held(0, j + k) for k in range(j)],
                    functools.partial(swap, mask=spread(j, inside)),
                )
            else:
                plan[f"p{j}"] = (
                    lambda top=top, lower=lower: [(get(f"c{top}"), lower, False)],
                    functools.partial(swap, mask=spread(lower, inside)),
                )
        for key in range(1, 2 * far):
            bit = key & -key
            before = key ^ bit
            sizes[key] = pieces[far if key >= far else 0]
            for i, js in enumerate(sizes[key]):
                if before:
                    source = lambda before=before, i=i: [get(f"s{before}.{i}")]
                else:
                    source = lambda js=js: [part(j) for j in js]
                plan[f"s{key}.{i}"] = (
                    source,
                    functools.partial(swap, mask=1 << outside[bit.bit_length() - 1]),
                )
        for key in sorted(range(1, group), key=lambda k: (bin(k).count("1"), k)):
            bit = key & -key
            before = key ^ bit
            name = f"r{key}"
            if before == 0:
                send = [j for j in range(group) if j ^ bit >= bit]
                joins[name] = jnp.concatenate([slices[j] for j in send], axis=0)
                source = lambda name=name: [done["i"][name]]
            elif before & (before - 1) == 0:
                send = orders[f"r{before}"]
                source = lambda before=before: [get(f"r{before}")]
                other = [j ^ before for j in range(1, group) if j ^ bit not in send]
                orders[f"u{key}"] = [j ^ before for j in other]
                plan[f"u{key}"] = (
                    lambda bit=bit, other=other: [held(bit, j) for j in other],
                    functools.partial(swap, mask=spread(before, inside)),
                )
            else:
                send = [j for j in range(group) if j != bit]
                source = lambda before=before, send=send: [held(before, j) for j in send]
            orders[name] = [j ^ bit for j in send]
            plan[name] = (source, functools.partial(swap, mask=spread(bit, inside)))

        def rows_of(key):
            top = key.bit_length() - 1
            first = (f"c{top}", list(range(key))) if key == 1 << top else (f"p{key}", [0])
            names = [name for name in (f"r{key}", f"u{key}") if name in plan]
            return [first] + [(name, orders[name]) for name in names]

        for shift in range(1, halves):
            turn = functools.partial(rotate, shift=shift)
            plan[f"t{shift}o"] = (lambda: [own], turn)
            for key in range(1, group):
                plan[f"t{shift}k{key}"] = (
                    lambda key=key: [
                        (get(name), i, False)
                        for name, order in rows_of(key)
                        for i in range(len(order))
                    ],
                    turn,
                )

        def projection(name, keys):
            values = []
            places = []
            for shift in range(halves):
                away = f"t{shift}" if shift else ""
                for place, key in enumerate(keys):
                    if key == 0:
                        values.append(in_vmem(get(away + "o")) if shift else in_hbm(own))
                        places.append((place, shift, [None] * group))
                        continue
                    if shift:
                        values.append(in_vmem(get(f"{away}k{key}")))
                        places.append((place, shift, sum([js for _, js in rows_of(key)], [])))
                        continue
                    for source, order in rows_of(key):
                        values.append(in_vmem(get(source)))
                        places.append((place, shift, order))
            return project(
                name, pos, cols, counts, potential, values, places, inside, halves
            )

        plan["q"] = (
            lambda: [projection("project", range(group - 1))],
            lambda value: value,
        )
        done["i"] = {
            "cols": block_cols.reshape(-1),
            "counts": block_counts.reshape(-1),
            "pairing": partners.reshape(-1),
            **joins,
        }
        done["i"] = lax.optimization_barrier((done["i"], get("c0")))[0]
        cols, counts, pairing = (done["i"][name] for name in ("cols", "counts", "pairing"))
        for name in WAITS:
            if name in plan:
                get(name)
        projected = get("q")
        projected_last = projection("project_last", [group - 1])
        early = [(part(j)[0], 1) for j in range(group)]
        for key in range(1, 2 * far - 1):
            early += [(get(f"s{key}.{i}"), len(js)) for i, js in enumerate(sizes[key])]
        key = 2 * far - 1
        late = [(get(f"s{key}.{i}"), len(js)) for i, js in enumerate(sizes[key])]
        total = couple(
            "couple",
            False,
            pos,
            pairing,
            [(projected, 0, early, None)],
            group,
            inside,
            outside,
            halves,
        )
        total = couple(
            "couple_last",
            True,
            pos,
            pairing,
            [(projected, 2 * far - 1, late, total), (projected_last, 0, early + late, None)],
            group,
            inside,
            outside,
            halves,
        )
        summed = total[0]
        for shift in range(1, halves):
            summed = summed + rotate(total[shift], shift)
        summed = summed.reshape((group, modes) + summed.shape[1:])
        result = summed[0]
        sent = summed.astype(jnp.bfloat16)
        for point in range(1, group):
            result = result + swap(sent[point], spread(point, inside)).astype(jnp.float32)
        return result[:, None] / gaps

    return jax.shard_map(
        per_device,
        mesh=mesh,
        in_specs=(
            P("ka", "orb", None),
            P(None, "orb", None, None, None),
            P(None, "orb", None),
            P(None, "orb"),
            P(),
            P(None, "ka", "orb", None),
        ),
        out_specs=P(None, "ka", "orb", None),
        check_vma=False,
    )
```

```python
import functools

import jax
import jax.numpy as jnp
from jax import lax
from jax.experimental import pallas as pl
from jax.experimental.pallas import tpu as pltpu
from jax.sharding import PartitionSpec as P

SPARE_VMEM = 6 * 2**20
SMEM = pl.BlockSpec(memory_space=pltpu.SMEM)
VMEM = pl.BlockSpec(memory_space=pltpu.VMEM)
ANY = pl.BlockSpec(memory_space=pl.ANY)


FIRST = ("c0", "c1", "s1.0")
SECOND = ("p3", "r1", "r2", "s2.1", "s1.1","s3.0","s1.2")
WAITS = {
    **dict.fromkeys(FIRST, ()),
    "s2.0": (),
    "t1o": ("s2.0",),
    "r1": ("c0","s1.0"),
    **dict.fromkeys(("p3", "r2", "s2.1", "s1.1"), FIRST+("i",)),
    **dict.fromkeys(("s3.0","s1.2"), ("p3",)),

    **dict.fromkeys(("s2.2","s3.1","r3","u3"), SECOND),
    **dict.fromkeys(("t1k1","t1k2"), SECOND),
    "q": (),
    "t1k3": ("q","s2.2","s3.1"),
}


def in_hbm(value):
    return pltpu.with_memory_space_constraint(value, pltpu.HBM)


def in_vmem(value):
    return pltpu.with_memory_space_constraint(value, pltpu.VMEM)


def split_bits(points, blocks):
    bits = points.bit_length() - 1
    inside = [bit for bit in range(bits) if bit % 2 == 0][: bits // 2]
    while blocks % (1 << len(inside)):
        inside.pop()
    return inside, [bit for bit in range(bits) if bit not in inside]


def spread(value, bits):
    return sum(((value >> i) & 1) << bit for i, bit in enumerate(bits))


def gathered(value, bits):
    return sum((((value >> bit) & 1) << i for i, bit in enumerate(bits)), 0 * value)


def stitch_kernel(places, *refs):
    sources, (out, sems) = refs[: len(places)], refs[len(places) :]
    rows = out.shape[0] // len(places)
    copies = []
    for i, (source, at) in enumerate(zip(sources, places)):
        copies.append(
            pltpu.make_async_copy(
                source.at[pl.ds(at * rows, rows)],
                out.at[pl.ds(i * rows, rows)],
                sems.at[i],
            )
        )
    for copy in copies:
        copy.start()
    for copy in copies:
        copy.wait()


def stitch(rows, sources, places):
    bands = sources[0].shape[1]
    return pl.pallas_call(
        functools.partial(stitch_kernel, places),
        out_shape=jax.ShapeDtypeStruct((len(places) * rows, bands), sources[0].dtype),
        in_specs=[ANY] * len(sources),
        out_specs=ANY,
        scratch_shapes=[pltpu.SemaphoreType.DMA((len(places),))],
        compiler_params=pltpu.CompilerParams(vmem_limit_bytes=2**20),
        cost_estimate=pl.CostEstimate(flops=0, bytes_accessed=0, transcendentals=0),
        name="stitch",
    )(*[in_vmem(source) for source in sources])


def project_kernel(orders, inside, halves, pos, cols, counts, potential, *refs):
    sources, (out, whole, blocks, sem, sems) = refs[:-5], refs[-5:]
    modes, rows, slots, size, _ = blocks.shape
    points, _, chunks, length, _ = whole.shape
    local_rows = potential.shape[1]
    chunk, half = gathered(pos[0], inside), pos[1]
    first = pltpu.make_async_copy(potential.at[:, pl.ds(chunk * rows, rows)], blocks, sem)
    first.start()
    copies = []
    for i, source in enumerate(sources):
        point, shift, order = orders[i]
        place = lax.rem(half + halves - shift, halves)
        for j, other in enumerate(order):
            copies.append(
                pltpu.make_async_copy(
                    source.at[pl.ds(j * length, length)],
                    whole.at[point, place, j if other is None else chunk ^ other],
                    sems.at[len(copies)],
                )
            )
    for copy in copies:
        copy.start()
    first.wait()
    for copy in copies:
        copy.wait()
    for mode in range(modes):
        for row in range(rows):
            at = mode * local_rows + chunk * rows + row
            used = counts[at]
            left = []
            right = []
            for slot in range(slots):
                block = blocks[mode, row, slot]
                left.append(jnp.where(slot < used, block, jnp.zeros_like(block)))
                col = cols[at * slots + slot]
                place = lax.div(col, local_rows)
                inner = lax.rem(col, local_rows)
                start = pl.multiple_of(lax.rem(inner, rows) * size, size)
                right.append(
                    jnp.concatenate(
                        [
                            whole[point, place, lax.div(inner, rows), pl.ds(start, size), :]
                            for point in range(points)
                        ],
                        axis=1,
                    )
                )
            product = jnp.dot(
                jnp.concatenate(left, axis=1),
                jnp.concatenate(right, axis=0),
                preferred_element_type=jnp.float32,
            )
            turned = product.astype(jnp.bfloat16).T
            for point in range(points):
                out[point * modes + mode, :, row * size : (row + 1) * size] = turned[
                    point * size : (point + 1) * size
                ]


def project(name, pos, cols, counts, potential, sources, orders, inside, halves):
    group = 1 << len(inside)
    modes, local_rows, slots, size, _ = potential.shape
    bands = sources[0].shape[1]
    rows = local_rows // group
    points = 1 + max(point for point, _, _ in orders)
    count = sum(len(order) for _, _, order in orders)
    held = 2 * size * (points * halves * local_rows * bands + modes * rows * slots * size)
    made = 2 * points * modes * bands * rows * size
    return pl.pallas_call(
        functools.partial(project_kernel, orders, inside, halves),
        out_shape=jax.ShapeDtypeStruct((points * modes, bands, rows * size), jnp.bfloat16),
        in_specs=[SMEM, SMEM, SMEM] + [ANY] * (1 + len(sources)),
        out_specs=VMEM,
        scratch_shapes=[
            pltpu.VMEM((points, halves, group, rows * size, bands), jnp.bfloat16),
            pltpu.VMEM((modes, rows, slots, size, size), jnp.bfloat16),
            pltpu.SemaphoreType.DMA,
            pltpu.SemaphoreType.DMA((count,)),
        ],
        compiler_params=pltpu.CompilerParams(vmem_limit_bytes=held + made + SPARE_VMEM),
        cost_estimate=pl.CostEstimate(flops=0, bytes_accessed=0, transcendentals=0),
        name=name,
    )(pos, cols, counts, in_hbm(potential), *sources)


def couple_kernel(jobs, last, inside, outside, halves, pos, partners, *refs):
    group = 1 << len(inside)
    points = group << len(outside)
    refs, (out, total) = refs[:-2], refs[-2:]
    me, half = pos[0], pos[1]
    for start, pairs, first, counts, resumed in jobs:
        projected, refs = refs[0], refs[1:]
        parts, refs = refs[: len(counts)], refs[len(counts) :]
        rows = projected.shape[2]
        modes = total.shape[0] // group
        if resumed:
            total[start : start + pairs] = refs[0][...]
            refs = refs[1:]
        else:
            total[start : start + pairs] = jnp.zeros((pairs,) + total.shape[1:], jnp.float32)

        def add(
            pair,
            carry,
            start=start,
            first=first,
            parts=tuple(zip(parts, counts)),
            projected=projected,
        ):
            point = lax.div(pair + start, modes)
            mine = me ^ spread(point, inside)
            away = partners[lax.rem(pair, modes) * points + mine] ^ me
            at = (gathered(away, outside) - first) * group + gathered(away, inside)
            base = 0
            for part, held in parts:
                here = at - base
                base += held

                @pl.when(jnp.logical_and(here >= 0, here < held))
                def _(part=part, here=here):
                    chunk = part[pl.ds(pl.multiple_of(here * rows, rows), rows), :]
                    total[pair + start] += jnp.dot(
                        projected[pair], chunk, preferred_element_type=jnp.float32
                    )

            return carry

        lax.fori_loop(0, pairs, add, 0)
    if last:
        bands = total.shape[1]
        share = bands // halves
        for pair in range(total.shape[0]):
            turned = total[pair].T
            for part in range(halves):
                out[lax.rem(part + halves - half, halves), pair] = turned[
                    part * share : (part + 1) * share
                ]
    else:
        out[...] = total[: out.shape[0]]


def couple(name, last, pos, partners, work, group, inside, outside, halves):
    jobs = []
    values = []
    start = 0
    for projected, first, parts, before in work:
        pairs, bands, rows = projected.shape
        jobs.append((start, pairs, first, [count for _, count in parts], before is not None))
        values += [projected] + [value for value, _ in parts]
        values += [] if before is None else [before]
        start += pairs
    total = start if last else (start // (group - 1)) * group if group > 1 else start
    shape = (halves, start, bands // halves, bands) if last else (start, bands, bands)
    held = sum(value.size * value.dtype.itemsize for value in values)
    held += 4 * (total + start) * bands * bands
    return pl.pallas_call(
        functools.partial(couple_kernel, jobs, last, inside, outside, halves),
        out_shape=jax.ShapeDtypeStruct(shape, jnp.float32),
        in_specs=[SMEM, SMEM] + [VMEM] * len(values),
        out_specs=VMEM,
        scratch_shapes=[pltpu.VMEM((total, bands, bands), jnp.float32)],
        compiler_params=pltpu.CompilerParams(vmem_limit_bytes=held + SPARE_VMEM),
        cost_estimate=pl.CostEstimate(flops=0, bytes_accessed=0, transcendentals=0),
        name=name,
    )(pos, partners, *[in_vmem(x) for x in values])


def solution(mesh):
    points = mesh.shape["ka"]
    halves = mesh.shape["orb"]

    def per_device(coefficients, potential, block_cols, block_counts, partners, gaps):
        modes, local_rows, _, _, _ = potential.shape
        inside, outside = split_bits(points, local_rows)
        group = 1 << len(inside)
        own = coefficients[0]
        rows = own.shape[0] // group
        me = lax.axis_index("ka").astype(jnp.int32)
        chunk = gathered(me, inside)
        pos = jnp.stack([me, lax.axis_index("orb").astype(jnp.int32)])
        pos, own = lax.optimization_barrier((pos, own))

        def swap(value, mask):
            return lax.ppermute(value, "ka", [(i, i ^ mask) for i in range(points)])

        def rotate(value, shift):
            return lax.ppermute(
                value, "orb", [(i, (i + shift) % halves) for i in range(halves)]
            )

        plan = {}
        done = {}

        def get(name):
            if name not in done:
                inputs, move = plan[name]
                inputs = [item if isinstance(item, tuple) else (item, None) for item in inputs()]
                places = [item[1:] for item in inputs]
                inputs = [item[0] for item in inputs]
                waits = [done[other] for other in WAITS.get(name, ()) if other in done]
                if waits:
                    inputs, _ = lax.optimization_barrier((inputs, waits))
                whole = places[0] == (None,)
                done[name] = move(inputs[0] if whole else joined(places, inputs))
            return done[name]

        far = 1 << (len(outside) - 1)
        pieces = {0: [[0], list(range(1, group - 1)), [group - 1]], far: [[0], list(range(1, group - 1)), [group - 1]]}
        sizes = {}
        orders = {}
        joins = {}

        slices = [
            lax.dynamic_slice_in_dim(own, (chunk ^ j) * rows, rows, 0) for j in range(group)
        ]

        def part(j):
            if j == 0:
                return slices[0], 0, False
            top = j.bit_length() - 1
            return (get(f"c{top}") if j == 1 << top else get(f"p{j}")), 0, False

        def held(key, j):
            if key == 0:
                return slices[j], 0, True
            for name in (f"r{key}", f"u{key}"):
                if j in orders.get(name, ()):
                    return get(name), orders[name].index(j), False
            return (get(f"c{key.bit_length() - 1}"), j, False) if j else part(key)

        def joined(places, values):
            if len(values) == 1 and values[0].shape[0] == rows:
                return values[0]
            if all(value.shape[0] == rows for value in values) and places[0] == (0, True):
                return jnp.concatenate(values, axis=0)
            return stitch(rows, values, [at for at, _ in places])

        for j in range(1, group):
            top = j.bit_length() - 1
            lower = j ^ (1 << top)
            if lower == 0:
                plan[f"c{top}"] = (
                    lambda j=j: [held(0, j + k) for k in range(j)],
                    functools.partial(swap, mask=spread(j, inside)),
                )
            else:
                plan[f"p{j}"] = (
                    lambda top=top, lower=lower: [(get(f"c{top}"), lower, False)],
                    functools.partial(swap, mask=spread(lower, inside)),
                )
        for key in range(1, 2 * far):
            bit = key & -key
            before = key ^ bit
            sizes[key] = pieces[far if key >= far else 0]
            for i, js in enumerate(sizes[key]):
                if before:
                    source = lambda before=before, i=i: [get(f"s{before}.{i}")]
                else:
                    source = lambda js=js: [part(j) for j in js]
                plan[f"s{key}.{i}"] = (
                    source,
                    functools.partial(swap, mask=1 << outside[bit.bit_length() - 1]),
                )
        for key in sorted(range(1, group), key=lambda k: (bin(k).count("1"), k)):
            bit = key & -key
            before = key ^ bit
            name = f"r{key}"
            if before == 0:
                send = [j for j in range(group) if j ^ bit >= bit]
                joins[name] = jnp.concatenate([slices[j] for j in send], axis=0)
                source = lambda name=name: [done["i"][name]]
            elif before & (before - 1) == 0:
                send = orders[f"r{before}"]
                source = lambda before=before: [get(f"r{before}")]
                other = [j ^ before for j in range(1, group) if j ^ bit not in send]
                orders[f"u{key}"] = [j ^ before for j in other]
                plan[f"u{key}"] = (
                    lambda bit=bit, other=other: [held(bit, j) for j in other],
                    functools.partial(swap, mask=spread(before, inside)),
                )
            else:
                send = [j for j in range(group) if j != bit]
                source = lambda before=before, send=send: [held(before, j) for j in send]
            orders[name] = [j ^ bit for j in send]
            plan[name] = (source, functools.partial(swap, mask=spread(bit, inside)))

        def rows_of(key):
            top = key.bit_length() - 1
            first = (f"c{top}", list(range(key))) if key == 1 << top else (f"p{key}", [0])
            names = [name for name in (f"r{key}", f"u{key}") if name in plan]
            return [first] + [(name, orders[name]) for name in names]

        for shift in range(1, halves):
            turn = functools.partial(rotate, shift=shift)
            plan[f"t{shift}o"] = (lambda: [own], turn)
            for key in range(1, group):
                plan[f"t{shift}k{key}"] = (
                    lambda key=key: [
                        (get(name), i, False)
                        for name, order in rows_of(key)
                        for i in range(len(order))
                    ],
                    turn,
                )

        def projection(name, keys):
            values = []
            places = []
            for shift in range(halves):
                away = f"t{shift}" if shift else ""
                for place, key in enumerate(keys):
                    if key == 0:
                        values.append(in_vmem(get(away + "o")) if shift else in_hbm(own))
                        places.append((place, shift, [None] * group))
                        continue
                    if shift:
                        values.append(in_vmem(get(f"{away}k{key}")))
                        places.append((place, shift, sum([js for _, js in rows_of(key)], [])))
                        continue
                    for source, order in rows_of(key):
                        values.append(in_vmem(get(source)))
                        places.append((place, shift, order))
            return project(
                name, pos, cols, counts, potential, values, places, inside, halves
            )

        plan["q"] = (
            lambda: [projection("project", range(group - 1))],
            lambda value: value,
        )
        done["i"] = {
            "cols": block_cols.reshape(-1),
            "counts": block_counts.reshape(-1),
            "pairing": partners.reshape(-1),
            **joins,
        }
        done["i"] = lax.optimization_barrier((done["i"], get("c0")))[0]
        cols, counts, pairing = (done["i"][name] for name in ("cols", "counts", "pairing"))
        for name in WAITS:
            if name in plan:
                get(name)
        projected = get("q")
        projected_last = projection("project_last", [group - 1])
        early = [(part(j)[0], 1) for j in range(group)]
        for key in range(1, 2 * far - 1):
            early += [(get(f"s{key}.{i}"), len(js)) for i, js in enumerate(sizes[key])]
        key = 2 * far - 1
        late = [(get(f"s{key}.{i}"), len(js)) for i, js in enumerate(sizes[key])]
        total = couple(
            "couple",
            False,
            pos,
            pairing,
            [(projected, 0, early, None)],
            group,
            inside,
            outside,
            halves,
        )
        total = couple(
            "couple_last",
            True,
            pos,
            pairing,
            [(projected, 2 * far - 1, late, total), (projected_last, 0, early + late, None)],
            group,
            inside,
            outside,
            halves,
        )
        summed = total[0]
        for shift in range(1, halves):
            summed = summed + rotate(total[shift], shift)
        summed = summed.reshape((group, modes) + summed.shape[1:])
        result = summed[0]
        sent = summed.astype(jnp.bfloat16)
        for point in range(1, group):
            result = result + swap(sent[point], spread(point, inside)).astype(jnp.float32)
        return result[:, None] / gaps

    return jax.shard_map(
        per_device,
        mesh=mesh,
        in_specs=(
            P("ka", "orb", None),
            P(None, "orb", None, None, None),
            P(None, "orb", None),
            P(None, "orb"),
            P(),
            P(None, "ka", "orb", None),
        ),
        out_specs=P(None, "ka", "orb", None),
        check_vma=False,
    )
```

```python
import functools

import jax
import jax.numpy as jnp
from jax import lax
from jax.experimental import pallas as pl
from jax.experimental.pallas import tpu as pltpu
from jax.sharding import PartitionSpec as P

SPARE_VMEM = 6 * 2**20
SMEM = pl.BlockSpec(memory_space=pltpu.SMEM)
VMEM = pl.BlockSpec(memory_space=pltpu.VMEM)
ANY = pl.BlockSpec(memory_space=pl.ANY)


FIRST = ("c0", "c1", "s1.0")
SECOND = ("p3","r1","r2","s1.1","s3.0","s2.2")
WAITS = {
    **dict.fromkeys(FIRST, ()),
    "s2.0": (),
    "s2.1": ("s2.0",),
    "t1o": ("s2.0",),
    "r1": ("c0", "s1.0"),
    **dict.fromkeys(("p3", "r2", "s1.1"), FIRST+("i","s2.0")),
    "s2.2": ("s2.1",),
    "s3.0": (),

    "s3.1": SECOND,
    **dict.fromkeys(("s2.3","r3","u3","s1.2"), SECOND),
    **dict.fromkeys(("t1k1","t1k2"), SECOND),
    "q": (),
    "t1k3": ("q","s2.3","s3.1","s1.2"),
}


def in_hbm(value):
    return pltpu.with_memory_space_constraint(value, pltpu.HBM)


def in_vmem(value):
    return pltpu.with_memory_space_constraint(value, pltpu.VMEM)


def split_bits(points, blocks):
    bits = points.bit_length() - 1
    inside = [bit for bit in range(bits) if bit % 2 == 0][: bits // 2]
    while blocks % (1 << len(inside)):
        inside.pop()
    return inside, [bit for bit in range(bits) if bit not in inside]


def spread(value, bits):
    return sum(((value >> i) & 1) << bit for i, bit in enumerate(bits))


def gathered(value, bits):
    return sum((((value >> bit) & 1) << i for i, bit in enumerate(bits)), 0 * value)


def stitch_kernel(places, *refs):
    sources, (out, sems) = refs[: len(places)], refs[len(places) :]
    rows = out.shape[0] // len(places)
    copies = []
    for i, (source, at) in enumerate(zip(sources, places)):
        copies.append(
            pltpu.make_async_copy(
                source.at[pl.ds(at * rows, rows)],
                out.at[pl.ds(i * rows, rows)],
                sems.at[i],
            )
        )
    for copy in copies:
        copy.start()
    for copy in copies:
        copy.wait()


def stitch(rows, sources, places):
    bands = sources[0].shape[1]
    return pl.pallas_call(
        functools.partial(stitch_kernel, places),
        out_shape=jax.ShapeDtypeStruct((len(places) * rows, bands), sources[0].dtype),
        in_specs=[ANY] * len(sources),
        out_specs=ANY,
        scratch_shapes=[pltpu.SemaphoreType.DMA((len(places),))],
        compiler_params=pltpu.CompilerParams(vmem_limit_bytes=2**20),
        cost_estimate=pl.CostEstimate(flops=0, bytes_accessed=0, transcendentals=0),
        name="stitch",
    )(*[in_vmem(source) for source in sources])


def project_kernel(orders, inside, halves, pos, cols, counts, potential, *refs):
    sources, (out, whole, blocks, sem, sems) = refs[:-5], refs[-5:]
    modes, rows, slots, size, _ = blocks.shape
    points, _, chunks, length, _ = whole.shape
    local_rows = potential.shape[1]
    chunk, half = gathered(pos[0], inside), pos[1]
    first = pltpu.make_async_copy(potential.at[:, pl.ds(chunk * rows, rows)], blocks, sem)
    first.start()
    copies = []
    for i, source in enumerate(sources):
        point, shift, order = orders[i]
        place = lax.rem(half + halves - shift, halves)
        for j, other in enumerate(order):
            copies.append(
                pltpu.make_async_copy(
                    source.at[pl.ds(j * length, length)],
                    whole.at[point, place, j if other is None else chunk ^ other],
                    sems.at[len(copies)],
                )
            )
    for copy in copies:
        copy.start()
    first.wait()
    for copy in copies:
        copy.wait()
    for mode in range(modes):
        for row in range(rows):
            at = mode * local_rows + chunk * rows + row
            used = counts[at]
            left = []
            right = []
            for slot in range(slots):
                block = blocks[mode, row, slot]
                left.append(jnp.where(slot < used, block, jnp.zeros_like(block)))
                col = cols[at * slots + slot]
                place = lax.div(col, local_rows)
                inner = lax.rem(col, local_rows)
                start = pl.multiple_of(lax.rem(inner, rows) * size, size)
                right.append(
                    jnp.concatenate(
                        [
                            whole[point, place, lax.div(inner, rows), pl.ds(start, size), :]
                            for point in range(points)
                        ],
                        axis=1,
                    )
                )
            product = jnp.dot(
                jnp.concatenate(left, axis=1),
                jnp.concatenate(right, axis=0),
                preferred_element_type=jnp.float32,
            )
            turned = product.astype(jnp.bfloat16).T
            for point in range(points):
                out[point * modes + mode, :, row * size : (row + 1) * size] = turned[
                    point * size : (point + 1) * size
                ]


def project(name, pos, cols, counts, potential, sources, orders, inside, halves):
    group = 1 << len(inside)
    modes, local_rows, slots, size, _ = potential.shape
    bands = sources[0].shape[1]
    rows = local_rows // group
    points = 1 + max(point for point, _, _ in orders)
    count = sum(len(order) for _, _, order in orders)
    held = 2 * size * (points * halves * local_rows * bands + modes * rows * slots * size)
    made = 2 * points * modes * bands * rows * size
    return pl.pallas_call(
        functools.partial(project_kernel, orders, inside, halves),
        out_shape=jax.ShapeDtypeStruct((points * modes, bands, rows * size), jnp.bfloat16),
        in_specs=[SMEM, SMEM, SMEM] + [ANY] * (1 + len(sources)),
        out_specs=VMEM,
        scratch_shapes=[
            pltpu.VMEM((points, halves, group, rows * size, bands), jnp.bfloat16),
            pltpu.VMEM((modes, rows, slots, size, size), jnp.bfloat16),
            pltpu.SemaphoreType.DMA,
            pltpu.SemaphoreType.DMA((count,)),
        ],
        compiler_params=pltpu.CompilerParams(vmem_limit_bytes=held + made + SPARE_VMEM),
        cost_estimate=pl.CostEstimate(flops=0, bytes_accessed=0, transcendentals=0),
        name=name,
    )(pos, cols, counts, in_hbm(potential), *sources)


def couple_kernel(jobs, last, inside, outside, halves, pos, partners, *refs):
    group = 1 << len(inside)
    points = group << len(outside)
    refs, (out, total) = refs[:-2], refs[-2:]
    me, half = pos[0], pos[1]
    for start, pairs, first, counts, resumed in jobs:
        projected, refs = refs[0], refs[1:]
        parts, refs = refs[: len(counts)], refs[len(counts) :]
        rows = projected.shape[2]
        modes = total.shape[0] // group
        if resumed:
            total[start : start + pairs] = refs[0][...]
            refs = refs[1:]
        else:
            total[start : start + pairs] = jnp.zeros((pairs,) + total.shape[1:], jnp.float32)

        def add(
            pair,
            carry,
            start=start,
            first=first,
            parts=tuple(zip(parts, counts)),
            projected=projected,
        ):
            point = lax.div(pair + start, modes)
            mine = me ^ spread(point, inside)
            away = partners[lax.rem(pair, modes) * points + mine] ^ me
            at = (gathered(away, outside) - first) * group + gathered(away, inside)
            base = 0
            for part, held in parts:
                here = at - base
                base += held

                @pl.when(jnp.logical_and(here >= 0, here < held))
                def _(part=part, here=here):
                    chunk = part[pl.ds(pl.multiple_of(here * rows, rows), rows), :]
                    total[pair + start] += jnp.dot(
                        projected[pair], chunk, preferred_element_type=jnp.float32
                    )

            return carry

        lax.fori_loop(0, pairs, add, 0)
    if last:
        bands = total.shape[1]
        share = bands // halves
        for pair in range(total.shape[0]):
            turned = total[pair].T
            for part in range(halves):
                out[lax.rem(part + halves - half, halves), pair] = turned[
                    part * share : (part + 1) * share
                ]
    else:
        out[...] = total[: out.shape[0]]


def couple(name, last, pos, partners, work, group, inside, outside, halves):
    jobs = []
    values = []
    start = 0
    for projected, first, parts, before in work:
        pairs, bands, rows = projected.shape
        jobs.append((start, pairs, first, [count for _, count in parts], before is not None))
        values += [projected] + [value for value, _ in parts]
        values += [] if before is None else [before]
        start += pairs
    total = start if last else (start // (group - 1)) * group if group > 1 else start
    shape = (halves, start, bands // halves, bands) if last else (start, bands, bands)
    held = sum(value.size * value.dtype.itemsize for value in values)
    held += 4 * (total + start) * bands * bands
    return pl.pallas_call(
        functools.partial(couple_kernel, jobs, last, inside, outside, halves),
        out_shape=jax.ShapeDtypeStruct(shape, jnp.float32),
        in_specs=[SMEM, SMEM] + [VMEM] * len(values),
        out_specs=VMEM,
        scratch_shapes=[pltpu.VMEM((total, bands, bands), jnp.float32)],
        compiler_params=pltpu.CompilerParams(vmem_limit_bytes=held + SPARE_VMEM),
        cost_estimate=pl.CostEstimate(flops=0, bytes_accessed=0, transcendentals=0),
        name=name,
    )(pos, partners, *[in_vmem(x) for x in values])


def solution(mesh):
    points = mesh.shape["ka"]
    halves = mesh.shape["orb"]

    def per_device(coefficients, potential, block_cols, block_counts, partners, gaps):
        modes, local_rows, _, _, _ = potential.shape
        inside, outside = split_bits(points, local_rows)
        group = 1 << len(inside)
        own = coefficients[0]
        rows = own.shape[0] // group
        me = lax.axis_index("ka").astype(jnp.int32)
        chunk = gathered(me, inside)
        pos = jnp.stack([me, lax.axis_index("orb").astype(jnp.int32)])
        pos, own = lax.optimization_barrier((pos, own))

        def swap(value, mask):
            return lax.ppermute(value, "ka", [(i, i ^ mask) for i in range(points)])

        def rotate(value, shift):
            return lax.ppermute(
                value, "orb", [(i, (i + shift) % halves) for i in range(halves)]
            )

        plan = {}
        done = {}

        def get(name):
            if name not in done:
                inputs, move = plan[name]
                inputs = [item if isinstance(item, tuple) else (item, None) for item in inputs()]
                places = [item[1:] for item in inputs]
                inputs = [item[0] for item in inputs]
                waits = [done[other] for other in WAITS.get(name, ()) if other in done]
                if waits:
                    inputs, _ = lax.optimization_barrier((inputs, waits))
                whole = places[0] == (None,)
                done[name] = move(inputs[0] if whole else joined(places, inputs))
            return done[name]

        far = 1 << (len(outside) - 1)
        pieces = [[0], list(range(1, group - 1)), [group - 1]]
        finer = [[0], [1], list(range(2, group - 1)), [group - 1]]
        sizes = {}
        orders = {}
        joins = {}

        slices = [
            lax.dynamic_slice_in_dim(own, (chunk ^ j) * rows, rows, 0) for j in range(group)
        ]

        def part(j):
            if j == 0:
                return slices[0], 0, False
            top = j.bit_length() - 1
            return (get(f"c{top}") if j == 1 << top else get(f"p{j}")), 0, False

        def held(key, j):
            if key == 0:
                return slices[j], 0, True
            for name in (f"r{key}", f"u{key}"):
                if j in orders.get(name, ()):
                    return get(name), orders[name].index(j), False
            return (get(f"c{key.bit_length() - 1}"), j, False) if j else part(key)

        def joined(places, values):
            if len(values) == 1 and values[0].shape[0] == rows:
                return values[0]
            if all(value.shape[0] == rows for value in values) and places[0] == (0, True):
                return jnp.concatenate(values, axis=0)
            return stitch(rows, values, [at for at, _ in places])

        for j in range(1, group):
            top = j.bit_length() - 1
            lower = j ^ (1 << top)
            if lower == 0:
                plan[f"c{top}"] = (
                    lambda j=j: [held(0, j + k) for k in range(j)],
                    functools.partial(swap, mask=spread(j, inside)),
                )
            else:
                plan[f"p{j}"] = (
                    lambda top=top, lower=lower: [(get(f"c{top}"), lower, False)],
                    functools.partial(swap, mask=spread(lower, inside)),
                )
        for key in range(1, 2 * far):
            bit = key & -key
            before = key ^ bit
            sizes[key] = finer if key == far else pieces
            for i, js in enumerate(sizes[key]):
                if before == far:
                    source = lambda js=js: [
                        (get(f"s{far}.{k}"), at, False)
                        for k, parts in enumerate(finer)
                        for at, j in enumerate(parts)
                        if j in js
                    ]
                elif before:
                    source = lambda before=before, i=i: [get(f"s{before}.{i}")]
                else:
                    source = lambda js=js: [part(j) for j in js]
                plan[f"s{key}.{i}"] = (
                    source,
                    functools.partial(swap, mask=1 << outside[bit.bit_length() - 1]),
                )
        for key in sorted(range(1, group), key=lambda k: (bin(k).count("1"), k)):
            bit = key & -key
            before = key ^ bit
            name = f"r{key}"
            if before == 0:
                send = [j for j in range(group) if j ^ bit >= bit]
                joins[name] = jnp.concatenate([slices[j] for j in send], axis=0)
                source = lambda name=name: [done["i"][name]]
            elif before & (before - 1) == 0:
                send = orders[f"r{before}"]
                source = lambda before=before: [get(f"r{before}")]
                other = [j ^ before for j in range(1, group) if j ^ bit not in send]
                orders[f"u{key}"] = [j ^ before for j in other]
                plan[f"u{key}"] = (
                    lambda bit=bit, other=other: [held(bit, j) for j in other],
                    functools.partial(swap, mask=spread(before, inside)),
                )
            else:
                send = [j for j in range(group) if j != bit]
                source = lambda before=before, send=send: [held(before, j) for j in send]
            orders[name] = [j ^ bit for j in send]
            plan[name] = (source, functools.partial(swap, mask=spread(bit, inside)))

        def rows_of(key):
            top = key.bit_length() - 1
            first = (f"c{top}", list(range(key))) if key == 1 << top else (f"p{key}", [0])
            names = [name for name in (f"r{key}", f"u{key}") if name in plan]
            return [first] + [(name, orders[name]) for name in names]

        for shift in range(1, halves):
            turn = functools.partial(rotate, shift=shift)
            plan[f"t{shift}o"] = (lambda: [own], turn)
            for key in range(1, group):
                plan[f"t{shift}k{key}"] = (
                    lambda key=key: [
                        (get(name), i, False)
                        for name, order in rows_of(key)
                        for i in range(len(order))
                    ],
                    turn,
                )

        def projection(name, keys):
            values = []
            places = []
            for shift in range(halves):
                away = f"t{shift}" if shift else ""
                for place, key in enumerate(keys):
                    if key == 0:
                        values.append(in_vmem(get(away + "o")) if shift else in_hbm(own))
                        places.append((place, shift, [None] * group))
                        continue
                    if shift:
                        values.append(in_vmem(get(f"{away}k{key}")))
                        places.append((place, shift, sum([js for _, js in rows_of(key)], [])))
                        continue
                    for source, order in rows_of(key):
                        values.append(in_vmem(get(source)))
                        places.append((place, shift, order))
            return project(
                name, pos, cols, counts, potential, values, places, inside, halves
            )

        plan["q"] = (
            lambda: [projection("project", range(group - 1))],
            lambda value: value,
        )
        done["i"] = {
            "cols": block_cols.reshape(-1),
            "counts": block_counts.reshape(-1),
            "pairing": partners.reshape(-1),
            **joins,
        }
        done["i"] = lax.optimization_barrier((done["i"], get("c0")))[0]
        cols, counts, pairing = (done["i"][name] for name in ("cols", "counts", "pairing"))
        for name in WAITS:
            if name in plan:
                get(name)
        projected = get("q")
        projected_last = projection("project_last", [group - 1])
        early = [(part(j)[0], 1) for j in range(group)]
        for key in range(1, 2 * far - 1):
            early += [(get(f"s{key}.{i}"), len(js)) for i, js in enumerate(sizes[key])]
        key = 2 * far - 1
        late = [(get(f"s{key}.{i}"), len(js)) for i, js in enumerate(sizes[key])]
        total = couple(
            "couple",
            False,
            pos,
            pairing,
            [(projected, 0, early, None)],
            group,
            inside,
            outside,
            halves,
        )
        total = couple(
            "couple_last",
            True,
            pos,
            pairing,
            [(projected, 2 * far - 1, late, total), (projected_last, 0, early + late, None)],
            group,
            inside,
            outside,
            halves,
        )
        summed = total[0]
        for shift in range(1, halves):
            summed = summed + rotate(total[shift], shift)
        summed = summed.reshape((group, modes) + summed.shape[1:])
        result = summed[0]
        sent = summed.astype(jnp.bfloat16)
        for point in range(1, group):
            result = result + swap(sent[point], spread(point, inside)).astype(jnp.float32)
        return result[:, None] / gaps

    return jax.shard_map(
        per_device,
        mesh=mesh,
        in_specs=(
            P("ka", "orb", None),
            P(None, "orb", None, None, None),
            P(None, "orb", None),
            P(None, "orb"),
            P(),
            P(None, "ka", "orb", None),
        ),
        out_specs=P(None, "ka", "orb", None),
        check_vma=False,
    )
```

```python
import functools

import jax
import jax.numpy as jnp
from jax import lax
from jax.experimental import pallas as pl
from jax.experimental.pallas import tpu as pltpu
from jax.sharding import PartitionSpec as P

SPARE_VMEM = 6 * 2**20
SMEM = pl.BlockSpec(memory_space=pltpu.SMEM)
VMEM = pl.BlockSpec(memory_space=pltpu.VMEM)
ANY = pl.BlockSpec(memory_space=pl.ANY)


FIRST = ("c0", "c1", "s1.0")
SECOND = ("p3","r1","r2","s1.1","s3.0","s2.2","s1.2")
WAITS = {
    **dict.fromkeys(FIRST, ()),
    "s2.0": (),
    "s2.1": ("s2.0",),
    "t1o": ("s2.0",),
    "r1": ("c0", "s1.0"),
    **dict.fromkeys(("p3", "r2", "s1.1"), FIRST+("i","s2.0")),
    "s2.2": ("s2.1",),
    "s3.0": (),
    "s1.2": ("p3","s3.0"),
    "s3.1": SECOND,
    **dict.fromkeys(("s2.3","r3","u3"), SECOND),
    **dict.fromkeys(("t1k1","t1k2"), SECOND),
    "q": (),
    "t1k3": ("q","s2.3","s3.1"),
}


def in_hbm(value):
    return pltpu.with_memory_space_constraint(value, pltpu.HBM)


def in_vmem(value):
    return pltpu.with_memory_space_constraint(value, pltpu.VMEM)


def split_bits(points, blocks):
    bits = points.bit_length() - 1
    inside = [bit for bit in range(bits) if bit % 2 == 0][: bits // 2]
    while blocks % (1 << len(inside)):
        inside.pop()
    return inside, [bit for bit in range(bits) if bit not in inside]


def spread(value, bits):
    return sum(((value >> i) & 1) << bit for i, bit in enumerate(bits))


def gathered(value, bits):
    return sum((((value >> bit) & 1) << i for i, bit in enumerate(bits)), 0 * value)


def stitch_kernel(places, *refs):
    sources, (out, sems) = refs[: len(places)], refs[len(places) :]
    rows = out.shape[0] // len(places)
    copies = []
    for i, (source, at) in enumerate(zip(sources, places)):
        copies.append(
            pltpu.make_async_copy(
                source.at[pl.ds(at * rows, rows)],
                out.at[pl.ds(i * rows, rows)],
                sems.at[i],
            )
        )
    for copy in copies:
        copy.start()
    for copy in copies:
        copy.wait()


def stitch(rows, sources, places):
    bands = sources[0].shape[1]
    return pl.pallas_call(
        functools.partial(stitch_kernel, places),
        out_shape=jax.ShapeDtypeStruct((len(places) * rows, bands), sources[0].dtype),
        in_specs=[ANY] * len(sources),
        out_specs=ANY,
        scratch_shapes=[pltpu.SemaphoreType.DMA((len(places),))],
        compiler_params=pltpu.CompilerParams(vmem_limit_bytes=2**20),
        cost_estimate=pl.CostEstimate(flops=0, bytes_accessed=0, transcendentals=0),
        name="stitch",
    )(*[in_vmem(source) for source in sources])


def project_kernel(orders, inside, halves, pos, cols, counts, potential, *refs):
    sources, (out, whole, blocks, sem, sems) = refs[:-5], refs[-5:]
    modes, rows, slots, size, _ = blocks.shape
    points, _, chunks, length, _ = whole.shape
    local_rows = potential.shape[1]
    chunk, half = gathered(pos[0], inside), pos[1]
    first = pltpu.make_async_copy(potential.at[:, pl.ds(chunk * rows, rows)], blocks, sem)
    first.start()
    copies = []
    for i, source in enumerate(sources):
        point, shift, order = orders[i]
        place = lax.rem(half + halves - shift, halves)
        for j, other in enumerate(order):
            copies.append(
                pltpu.make_async_copy(
                    source.at[pl.ds(j * length, length)],
                    whole.at[point, place, j if other is None else chunk ^ other],
                    sems.at[len(copies)],
                )
            )
    for copy in copies:
        copy.start()
    first.wait()
    for copy in copies:
        copy.wait()
    for mode in range(modes):
        for row in range(rows):
            at = mode * local_rows + chunk * rows + row
            used = counts[at]
            left = []
            right = []
            for slot in range(slots):
                block = blocks[mode, row, slot]
                left.append(jnp.where(slot < used, block, jnp.zeros_like(block)))
                col = cols[at * slots + slot]
                place = lax.div(col, local_rows)
                inner = lax.rem(col, local_rows)
                start = pl.multiple_of(lax.rem(inner, rows) * size, size)
                right.append(
                    jnp.concatenate(
                        [
                            whole[point, place, lax.div(inner, rows), pl.ds(start, size), :]
                            for point in range(points)
                        ],
                        axis=1,
                    )
                )
            product = jnp.dot(
                jnp.concatenate(left, axis=1),
                jnp.concatenate(right, axis=0),
                preferred_element_type=jnp.float32,
            )
            turned = product.astype(jnp.bfloat16).T
            for point in range(points):
                out[point * modes + mode, :, row * size : (row + 1) * size] = turned[
                    point * size : (point + 1) * size
                ]


def project(name, pos, cols, counts, potential, sources, orders, inside, halves):
    group = 1 << len(inside)
    modes, local_rows, slots, size, _ = potential.shape
    bands = sources[0].shape[1]
    rows = local_rows // group
    points = 1 + max(point for point, _, _ in orders)
    count = sum(len(order) for _, _, order in orders)
    held = 2 * size * (points * halves * local_rows * bands + modes * rows * slots * size)
    made = 2 * points * modes * bands * rows * size
    return pl.pallas_call(
        functools.partial(project_kernel, orders, inside, halves),
        out_shape=jax.ShapeDtypeStruct((points * modes, bands, rows * size), jnp.bfloat16),
        in_specs=[SMEM, SMEM, SMEM] + [ANY] * (1 + len(sources)),
        out_specs=VMEM,
        scratch_shapes=[
            pltpu.VMEM((points, halves, group, rows * size, bands), jnp.bfloat16),
            pltpu.VMEM((modes, rows, slots, size, size), jnp.bfloat16),
            pltpu.SemaphoreType.DMA,
            pltpu.SemaphoreType.DMA((count,)),
        ],
        compiler_params=pltpu.CompilerParams(vmem_limit_bytes=held + made + SPARE_VMEM),
        cost_estimate=pl.CostEstimate(flops=0, bytes_accessed=0, transcendentals=0),
        name=name,
    )(pos, cols, counts, in_hbm(potential), *sources)


def couple_kernel(jobs, last, inside, outside, halves, pos, partners, *refs):
    group = 1 << len(inside)
    points = group << len(outside)
    refs, (out, total) = refs[:-2], refs[-2:]
    me, half = pos[0], pos[1]
    for start, pairs, first, counts, resumed in jobs:
        projected, refs = refs[0], refs[1:]
        parts, refs = refs[: len(counts)], refs[len(counts) :]
        rows = projected.shape[2]
        modes = total.shape[0] // group
        if resumed:
            total[start : start + pairs] = refs[0][...]
            refs = refs[1:]
        else:
            total[start : start + pairs] = jnp.zeros((pairs,) + total.shape[1:], jnp.float32)

        def add(
            pair,
            carry,
            start=start,
            first=first,
            parts=tuple(zip(parts, counts)),
            projected=projected,
        ):
            point = lax.div(pair + start, modes)
            mine = me ^ spread(point, inside)
            away = partners[lax.rem(pair, modes) * points + mine] ^ me
            at = (gathered(away, outside) - first) * group + gathered(away, inside)
            base = 0
            for part, held in parts:
                here = at - base
                base += held

                @pl.when(jnp.logical_and(here >= 0, here < held))
                def _(part=part, here=here):
                    chunk = part[pl.ds(pl.multiple_of(here * rows, rows), rows), :]
                    total[pair + start] += jnp.dot(
                        projected[pair], chunk, preferred_element_type=jnp.float32
                    )

            return carry

        lax.fori_loop(0, pairs, add, 0)
    if last:
        bands = total.shape[1]
        share = bands // halves
        for pair in range(total.shape[0]):
            turned = total[pair].T
            for part in range(halves):
                out[lax.rem(part + halves - half, halves), pair] = turned[
                    part * share : (part + 1) * share
                ]
    else:
        out[...] = total[: out.shape[0]]


def couple(name, last, pos, partners, work, group, inside, outside, halves):
    jobs = []
    values = []
    start = 0
    for projected, first, parts, before in work:
        pairs, bands, rows = projected.shape
        jobs.append((start, pairs, first, [count for _, count in parts], before is not None))
        values += [projected] + [value for value, _ in parts]
        values += [] if before is None else [before]
        start += pairs
    total = start if last else (start // (group - 1)) * group if group > 1 else start
    shape = (halves, start, bands // halves, bands) if last else (start, bands, bands)
    held = sum(value.size * value.dtype.itemsize for value in values)
    held += 4 * (total + start) * bands * bands
    return pl.pallas_call(
        functools.partial(couple_kernel, jobs, last, inside, outside, halves),
        out_shape=jax.ShapeDtypeStruct(shape, jnp.float32),
        in_specs=[SMEM, SMEM] + [VMEM] * len(values),
        out_specs=VMEM,
        scratch_shapes=[pltpu.VMEM((total, bands, bands), jnp.float32)],
        compiler_params=pltpu.CompilerParams(vmem_limit_bytes=held + SPARE_VMEM),
        cost_estimate=pl.CostEstimate(flops=0, bytes_accessed=0, transcendentals=0),
        name=name,
    )(pos, partners, *[in_vmem(x) for x in values])


def solution(mesh):
    points = mesh.shape["ka"]
    halves = mesh.shape["orb"]

    def per_device(coefficients, potential, block_cols, block_counts, partners, gaps):
        modes, local_rows, _, _, _ = potential.shape
        inside, outside = split_bits(points, local_rows)
        group = 1 << len(inside)
        own = coefficients[0]
        rows = own.shape[0] // group
        me = lax.axis_index("ka").astype(jnp.int32)
        chunk = gathered(me, inside)
        pos = jnp.stack([me, lax.axis_index("orb").astype(jnp.int32)])
        pos, own = lax.optimization_barrier((pos, own))

        def swap(value, mask):
            return lax.ppermute(value, "ka", [(i, i ^ mask) for i in range(points)])

        def rotate(value, shift):
            return lax.ppermute(
                value, "orb", [(i, (i + shift) % halves) for i in range(halves)]
            )

        plan = {}
        done = {}

        def get(name):
            if name not in done:
                inputs, move = plan[name]
                inputs = [item if isinstance(item, tuple) else (item, None) for item in inputs()]
                places = [item[1:] for item in inputs]
                inputs = [item[0] for item in inputs]
                waits = [done[other] for other in WAITS.get(name, ()) if other in done]
                if waits:
                    inputs, _ = lax.optimization_barrier((inputs, waits))
                whole = places[0] == (None,)
                done[name] = move(inputs[0] if whole else joined(places, inputs))
            return done[name]

        far = 1 << (len(outside) - 1)
        pieces = [[0], list(range(1, group - 1)), [group - 1]]
        finer = [[0], [1], list(range(2, group - 1)), [group - 1]]
        sizes = {}
        orders = {}
        joins = {}

        slices = [
            lax.dynamic_slice_in_dim(own, (chunk ^ j) * rows, rows, 0) for j in range(group)
        ]

        def part(j):
            if j == 0:
                return slices[0], 0, False
            top = j.bit_length() - 1
            return (get(f"c{top}") if j == 1 << top else get(f"p{j}")), 0, False

        def held(key, j):
            if key == 0:
                return slices[j], 0, True
            for name in (f"r{key}", f"u{key}"):
                if j in orders.get(name, ()):
                    return get(name), orders[name].index(j), False
            return (get(f"c{key.bit_length() - 1}"), j, False) if j else part(key)

        def joined(places, values):
            if len(values) == 1 and values[0].shape[0] == rows:
                return values[0]
            if all(value.shape[0] == rows for value in values) and places[0] == (0, True):
                return jnp.concatenate(values, axis=0)
            return stitch(rows, values, [at for at, _ in places])

        for j in range(1, group):
            top = j.bit_length() - 1
            lower = j ^ (1 << top)
            if lower == 0:
                plan[f"c{top}"] = (
                    lambda j=j: [held(0, j + k) for k in range(j)],
                    functools.partial(swap, mask=spread(j, inside)),
                )
            else:
                plan[f"p{j}"] = (
                    lambda top=top, lower=lower: [(get(f"c{top}"), lower, False)],
                    functools.partial(swap, mask=spread(lower, inside)),
                )
        for key in range(1, 2 * far):
            bit = key & -key
            before = key ^ bit
            sizes[key] = finer if key == far else pieces
            for i, js in enumerate(sizes[key]):
                if before == far:
                    source = lambda js=js: [
                        (get(f"s{far}.{k}"), at, False)
                        for k, parts in enumerate(finer)
                        for at, j in enumerate(parts)
                        if j in js
                    ]
                elif before:
                    source = lambda before=before, i=i: [get(f"s{before}.{i}")]
                else:
                    source = lambda js=js: [part(j) for j in js]
                plan[f"s{key}.{i}"] = (
                    source,
                    functools.partial(swap, mask=1 << outside[bit.bit_length() - 1]),
                )
        for key in sorted(range(1, group), key=lambda k: (bin(k).count("1"), k)):
            bit = key & -key
            before = key ^ bit
            name = f"r{key}"
            if before == 0:
                send = [j for j in range(group) if j ^ bit >= bit]
                joins[name] = jnp.concatenate([slices[j] for j in send], axis=0)
                source = lambda name=name: [done["i"][name]]
            elif before & (before - 1) == 0:
                send = orders[f"r{before}"]
                source = lambda before=before: [get(f"r{before}")]
                other = [j ^ before for j in range(1, group) if j ^ bit not in send]
                orders[f"u{key}"] = [j ^ before for j in other]
                plan[f"u{key}"] = (
                    lambda bit=bit, other=other: [held(bit, j) for j in other],
                    functools.partial(swap, mask=spread(before, inside)),
                )
            else:
                send = [j for j in range(group) if j != bit]
                source = lambda before=before, send=send: [held(before, j) for j in send]
            orders[name] = [j ^ bit for j in send]
            plan[name] = (source, functools.partial(swap, mask=spread(bit, inside)))

        def rows_of(key):
            top = key.bit_length() - 1
            first = (f"c{top}", list(range(key))) if key == 1 << top else (f"p{key}", [0])
            names = [name for name in (f"r{key}", f"u{key}") if name in plan]
            return [first] + [(name, orders[name]) for name in names]

        for shift in range(1, halves):
            turn = functools.partial(rotate, shift=shift)
            plan[f"t{shift}o"] = (lambda: [own], turn)
            for key in range(1, group):
                plan[f"t{shift}k{key}"] = (
                    lambda key=key: [
                        (get(name), i, False)
                        for name, order in rows_of(key)
                        for i in range(len(order))
                    ],
                    turn,
                )

        def projection(name, keys):
            values = []
            places = []
            for shift in range(halves):
                away = f"t{shift}" if shift else ""
                for place, key in enumerate(keys):
                    if key == 0:
                        values.append(in_vmem(get(away + "o")) if shift else in_hbm(own))
                        places.append((place, shift, [None] * group))
                        continue
                    if shift:
                        values.append(in_vmem(get(f"{away}k{key}")))
                        places.append((place, shift, sum([js for _, js in rows_of(key)], [])))
                        continue
                    for source, order in rows_of(key):
                        values.append(in_vmem(get(source)))
                        places.append((place, shift, order))
            return project(
                name, pos, cols, counts, potential, values, places, inside, halves
            )

        plan["q"] = (
            lambda: [projection("project", range(group - 1))],
            lambda value: value,
        )
        done["i"] = {
            "cols": block_cols.reshape(-1),
            "counts": block_counts.reshape(-1),
            "pairing": partners.reshape(-1),
            **joins,
        }
        done["i"] = lax.optimization_barrier((done["i"], get("c0")))[0]
        cols, counts, pairing = (done["i"][name] for name in ("cols", "counts", "pairing"))
        for name in WAITS:
            if name in plan:
                get(name)
        projected = get("q")
        projected_last = projection("project_last", [group - 1])
        early = [(part(j)[0], 1) for j in range(group)]
        for key in range(1, 2 * far - 1):
            early += [(get(f"s{key}.{i}"), len(js)) for i, js in enumerate(sizes[key])]
        key = 2 * far - 1
        late = [(get(f"s{key}.{i}"), len(js)) for i, js in enumerate(sizes[key])]
        total = couple(
            "couple",
            False,
            pos,
            pairing,
            [(projected, 0, early, None)],
            group,
            inside,
            outside,
            halves,
        )
        total = couple(
            "couple_last",
            True,
            pos,
            pairing,
            [(projected, 2 * far - 1, late, total), (projected_last, 0, early + late, None)],
            group,
            inside,
            outside,
            halves,
        )
        summed = total[0]
        for shift in range(1, halves):
            summed = summed + rotate(total[shift], shift)
        summed = summed.reshape((group, modes) + summed.shape[1:])
        result = summed[0]
        sent = summed.astype(jnp.bfloat16)
        for point in range(1, group):
            result = result + swap(sent[point], spread(point, inside)).astype(jnp.float32)
        return result[:, None] / gaps

    return jax.shard_map(
        per_device,
        mesh=mesh,
        in_specs=(
            P("ka", "orb", None),
            P(None, "orb", None, None, None),
            P(None, "orb", None),
            P(None, "orb"),
            P(),
            P(None, "ka", "orb", None),
        ),
        out_specs=P(None, "ka", "orb", None),
        check_vma=False,
    )
```

```python
import functools

import jax
import jax.numpy as jnp
from jax import lax
from jax.experimental import pallas as pl
from jax.experimental.pallas import tpu as pltpu
from jax.sharding import PartitionSpec as P

SPARE_VMEM = 6 * 2**20
SMEM = pl.BlockSpec(memory_space=pltpu.SMEM)
VMEM = pl.BlockSpec(memory_space=pltpu.VMEM)
ANY = pl.BlockSpec(memory_space=pl.ANY)


FIRST = ("c0", "c1", "s1.0")
SECOND = ("p3","r1","r2","s1.1","s3.0","s2.2","s1.2")
WAITS = {
    **dict.fromkeys(FIRST, ()),
    "s2.0": (),
    "s2.1": ("s2.0",),
    "t1o": ("s2.0",),
    "r1": ("c0", "s1.0"),
    **dict.fromkeys(("p3", "r2", "s1.1"), FIRST+("i","s2.0")),
    "s2.2": ("s2.1",),
    "s3.0": (),
    "s1.2": ("p3","s3.0"),
    "s3.1": SECOND,
    **dict.fromkeys(("s2.3","r3","u3"), SECOND),
    **dict.fromkeys(("t1k1","t1k2"), SECOND),
    "q": (),
    "t1k3": ("q","s2.3","s3.1"),
}


def in_hbm(value):
    return pltpu.with_memory_space_constraint(value, pltpu.HBM)


def in_vmem(value):
    return pltpu.with_memory_space_constraint(value, pltpu.VMEM)


def split_bits(points, blocks):
    bits = points.bit_length() - 1
    inside = [bit for bit in range(bits) if bit % 2 == 0][: bits // 2]
    while blocks % (1 << len(inside)):
        inside.pop()
    return inside, [bit for bit in range(bits) if bit not in inside]


def spread(value, bits):
    return sum(((value >> i) & 1) << bit for i, bit in enumerate(bits))


def gathered(value, bits):
    return sum((((value >> bit) & 1) << i for i, bit in enumerate(bits)), 0 * value)


def stitch_kernel(places, *refs):
    sources, (out, sems) = refs[: len(places)], refs[len(places) :]
    rows = out.shape[0] // len(places)
    copies = []
    for i, (source, at) in enumerate(zip(sources, places)):
        copies.append(
            pltpu.make_async_copy(
                source.at[pl.ds(at * rows, rows)],
                out.at[pl.ds(i * rows, rows)],
                sems.at[i],
            )
        )
    for copy in copies:
        copy.start()
    for copy in copies:
        copy.wait()


def stitch(rows, sources, places):
    bands = sources[0].shape[1]
    return pl.pallas_call(
        functools.partial(stitch_kernel, places),
        out_shape=jax.ShapeDtypeStruct((len(places) * rows, bands), sources[0].dtype),
        in_specs=[ANY] * len(sources),
        out_specs=ANY,
        scratch_shapes=[pltpu.SemaphoreType.DMA((len(places),))],
        compiler_params=pltpu.CompilerParams(vmem_limit_bytes=2**20),
        cost_estimate=pl.CostEstimate(flops=0, bytes_accessed=0, transcendentals=0),
        name="stitch",
    )(*[in_vmem(source) for source in sources])


def project_kernel(orders, inside, halves, pos, cols, counts, potential, *refs):
    sources, (out, whole, blocks, sem, sems) = refs[:-5], refs[-5:]
    modes, rows, slots, size, _ = blocks.shape
    points, _, chunks, length, _ = whole.shape
    local_rows = potential.shape[1]
    chunk, half = gathered(pos[0], inside), pos[1]
    first = pltpu.make_async_copy(potential.at[:, pl.ds(chunk * rows, rows)], blocks, sem)
    first.start()
    copies = []
    for i, source in enumerate(sources):
        point, shift, order = orders[i]
        place = lax.rem(half + halves - shift, halves)
        for j, other in enumerate(order):
            copies.append(
                pltpu.make_async_copy(
                    source.at[pl.ds(j * length, length)],
                    whole.at[point, place, j if other is None else chunk ^ other],
                    sems.at[len(copies)],
                )
            )
    for copy in copies:
        copy.start()
    first.wait()
    for copy in copies:
        copy.wait()
    for mode in range(modes):
        for row in range(rows):
            at = mode * local_rows + chunk * rows + row
            used = counts[at]
            left = []
            right = []
            for slot in range(slots):
                block = blocks[mode, row, slot]
                left.append(jnp.where(slot < used, block, jnp.zeros_like(block)))
                col = cols[at * slots + slot]
                place = lax.div(col, local_rows)
                inner = lax.rem(col, local_rows)
                start = pl.multiple_of(lax.rem(inner, rows) * size, size)
                right.append(
                    jnp.concatenate(
                        [
                            whole[point, place, lax.div(inner, rows), pl.ds(start, size), :]
                            for point in range(points)
                        ],
                        axis=1,
                    )
                )
            product = jnp.dot(
                jnp.concatenate(left, axis=1),
                jnp.concatenate(right, axis=0),
                preferred_element_type=jnp.float32,
            )
            turned = product.astype(jnp.bfloat16).T
            for point in range(points):
                out[point * modes + mode, :, row * size : (row + 1) * size] = turned[
                    point * size : (point + 1) * size
                ]


def project(name, pos, cols, counts, potential, sources, orders, inside, halves):
    group = 1 << len(inside)
    modes, local_rows, slots, size, _ = potential.shape
    bands = sources[0].shape[1]
    rows = local_rows // group
    points = 1 + max(point for point, _, _ in orders)
    count = sum(len(order) for _, _, order in orders)
    held = 2 * size * (points * halves * local_rows * bands + modes * rows * slots * size)
    made = 2 * points * modes * bands * rows * size
    return pl.pallas_call(
        functools.partial(project_kernel, orders, inside, halves),
        out_shape=jax.ShapeDtypeStruct((points * modes, bands, rows * size), jnp.bfloat16),
        in_specs=[SMEM, SMEM, SMEM] + [ANY] * (1 + len(sources)),
        out_specs=VMEM,
        scratch_shapes=[
            pltpu.VMEM((points, halves, group, rows * size, bands), jnp.bfloat16),
            pltpu.VMEM((modes, rows, slots, size, size), jnp.bfloat16),
            pltpu.SemaphoreType.DMA,
            pltpu.SemaphoreType.DMA((count,)),
        ],
        compiler_params=pltpu.CompilerParams(vmem_limit_bytes=held + made + SPARE_VMEM),
        cost_estimate=pl.CostEstimate(flops=0, bytes_accessed=0, transcendentals=0),
        name=name,
    )(pos, cols, counts, in_hbm(potential), *sources)


def couple_kernel(jobs, last, inside, outside, halves, pos, partners, *refs):
    group = 1 << len(inside)
    points = group << len(outside)
    refs, (out, total) = refs[:-2], refs[-2:]
    me, half = pos[0], pos[1]
    for start, pairs, first, counts, resumed in jobs:
        projected, refs = refs[0], refs[1:]
        parts, refs = refs[: len(counts)], refs[len(counts) :]
        rows = projected.shape[2]
        modes = total.shape[0] // group
        if resumed:
            total[start : start + pairs] = refs[0][...]
            refs = refs[1:]
        else:
            total[start : start + pairs] = jnp.zeros((pairs,) + total.shape[1:], jnp.float32)

        def add(
            pair,
            carry,
            start=start,
            first=first,
            parts=tuple(zip(parts, counts)),
            projected=projected,
        ):
            point = lax.div(pair + start, modes)
            mine = me ^ spread(point, inside)
            away = partners[lax.rem(pair, modes) * points + mine] ^ me
            at = (gathered(away, outside) - first) * group + gathered(away, inside)
            base = 0
            for part, held in parts:
                here = at - base
                base += held

                @pl.when(jnp.logical_and(here >= 0, here < held))
                def _(part=part, here=here):
                    chunk = part[pl.ds(pl.multiple_of(here * rows, rows), rows), :]
                    total[pair + start] += jnp.dot(
                        projected[pair], chunk, preferred_element_type=jnp.float32
                    )

            return carry

        lax.fori_loop(0, pairs, add, 0)
    if last:
        bands = total.shape[1]
        share = bands // halves
        for pair in range(total.shape[0]):
            turned = total[pair].T
            for part in range(halves):
                out[lax.rem(part + halves - half, halves), pair] = turned[
                    part * share : (part + 1) * share
                ]
    else:
        out[...] = total[: out.shape[0]]


def couple(name, last, pos, partners, work, group, inside, outside, halves):
    jobs = []
    values = []
    start = 0
    for projected, first, parts, before in work:
        pairs, bands, rows = projected.shape
        jobs.append((start, pairs, first, [count for _, count in parts], before is not None))
        values += [projected] + [value for value, _ in parts]
        values += [] if before is None else [before]
        start += pairs
    total = start if last else (start // (group - 1)) * group if group > 1 else start
    shape = (halves, start, bands // halves, bands) if last else (start, bands, bands)
    held = sum(value.size * value.dtype.itemsize for value in values)
    held += 4 * (total + start) * bands * bands
    return pl.pallas_call(
        functools.partial(couple_kernel, jobs, last, inside, outside, halves),
        out_shape=jax.ShapeDtypeStruct(shape, jnp.float32),
        in_specs=[SMEM, SMEM] + [VMEM] * len(values),
        out_specs=VMEM,
        scratch_shapes=[pltpu.VMEM((total, bands, bands), jnp.float32)],
        compiler_params=pltpu.CompilerParams(vmem_limit_bytes=held + SPARE_VMEM),
        cost_estimate=pl.CostEstimate(flops=0, bytes_accessed=0, transcendentals=0),
        name=name,
    )(pos, partners, *[in_vmem(x) for x in values])


def solution(mesh):
    points = mesh.shape["ka"]
    halves = mesh.shape["orb"]

    def per_device(coefficients, potential, block_cols, block_counts, partners, gaps):
        modes, local_rows, _, _, _ = potential.shape
        inside, outside = split_bits(points, local_rows)
        group = 1 << len(inside)
        own = coefficients[0]
        rows = own.shape[0] // group
        me = lax.axis_index("ka").astype(jnp.int32)
        chunk = gathered(me, inside)
        pos = jnp.stack([me, lax.axis_index("orb").astype(jnp.int32)])
        pos, own = lax.optimization_barrier((pos, own))

        def swap(value, mask):
            return lax.ppermute(value, "ka", [(i, i ^ mask) for i in range(points)])

        def rotate(value, shift):
            return lax.ppermute(
                value, "orb", [(i, (i + shift) % halves) for i in range(halves)]
            )

        plan = {}
        done = {}

        def get(name):
            if name not in done:
                inputs, move = plan[name]
                inputs = [item if isinstance(item, tuple) else (item, None) for item in inputs()]
                places = [item[1:] for item in inputs]
                inputs = [item[0] for item in inputs]
                waits = [done[other] for other in WAITS.get(name, ()) if other in done]
                if waits:
                    inputs, _ = lax.optimization_barrier((inputs, waits))
                whole = places[0] == (None,)
                done[name] = move(inputs[0] if whole else joined(places, inputs))
            return done[name]

        far = 1 << (len(outside) - 1)
        pieces = [[0], list(range(1, group - 1)), [group - 1]]
        finer = [[0], [1], list(range(2, group - 1)), [group - 1]]
        sizes = {}
        orders = {}
        joins = {}

        slices = [
            lax.dynamic_slice_in_dim(own, (chunk ^ j) * rows, rows, 0) for j in range(group)
        ]

        def part(j):
            if j == 0:
                return slices[0], 0, False
            top = j.bit_length() - 1
            return (get(f"c{top}") if j == 1 << top else get(f"p{j}")), 0, False

        def held(key, j):
            if key == 0:
                return slices[j], 0, True
            for name in (f"r{key}", f"u{key}"):
                if j in orders.get(name, ()):
                    return get(name), orders[name].index(j), False
            return (get(f"c{key.bit_length() - 1}"), j, False) if j else part(key)

        def joined(places, values):
            if len(values) == 1 and values[0].shape[0] == rows:
                return values[0]
            if all(value.shape[0] == rows for value in values) and places[0] == (0, True):
                return jnp.concatenate(values, axis=0)
            return stitch(rows, values, [at for at, _ in places])

        for j in range(1, group):
            top = j.bit_length() - 1
            lower = j ^ (1 << top)
            if lower == 0:
                plan[f"c{top}"] = (
                    lambda j=j: [held(0, j + k) for k in range(j)],
                    functools.partial(swap, mask=spread(j, inside)),
                )
            else:
                plan[f"p{j}"] = (
                    lambda top=top, lower=lower: [(get(f"c{top}"), lower, False)],
                    functools.partial(swap, mask=spread(lower, inside)),
                )
        for key in range(1, 2 * far):
            bit = key & -key
            before = key ^ bit
            sizes[key] = finer if key == far else pieces
            for i, js in enumerate(sizes[key]):
                if before == far:
                    source = lambda js=js: [
                        (get(f"s{far}.{k}"), at, False)
                        for k, parts in enumerate(finer)
                        for at, j in enumerate(parts)
                        if j in js
                    ]
                elif before:
                    source = lambda before=before, i=i: [get(f"s{before}.{i}")]
                else:
                    source = lambda js=js: [part(j) for j in js]
                plan[f"s{key}.{i}"] = (
                    source,
                    functools.partial(swap, mask=1 << outside[bit.bit_length() - 1]),
                )
        for key in sorted(range(1, group), key=lambda k: (bin(k).count("1"), k)):
            bit = key & -key
            before = key ^ bit
            name = f"r{key}"
            if before == 0:
                send = [j for j in range(group) if j ^ bit >= bit]
                joins[name] = jnp.concatenate([slices[j] for j in send], axis=0)
                source = lambda name=name: [done["i"][name]]
            elif before & (before - 1) == 0:
                send = orders[f"r{before}"]
                source = lambda before=before: [get(f"r{before}")]
                other = [j ^ before for j in range(1, group) if j ^ bit not in send]
                orders[f"u{key}"] = [j ^ before for j in other]
                plan[f"u{key}"] = (
                    lambda bit=bit, other=other: [held(bit, j) for j in other],
                    functools.partial(swap, mask=spread(before, inside)),
                )
            else:
                send = [j for j in range(group) if j != bit]
                source = lambda before=before, send=send: [held(before, j) for j in send]
            orders[name] = [j ^ bit for j in send]
            plan[name] = (source, functools.partial(swap, mask=spread(bit, inside)))

        def rows_of(key):
            top = key.bit_length() - 1
            first = (f"c{top}", list(range(key))) if key == 1 << top else (f"p{key}", [0])
            names = [name for name in (f"r{key}", f"u{key}") if name in plan]
            return [first] + [(name, orders[name]) for name in names]

        for shift in range(1, halves):
            turn = functools.partial(rotate, shift=shift)
            plan[f"t{shift}o"] = (lambda: [own], turn)
            for key in range(1, group):
                plan[f"t{shift}k{key}"] = (
                    lambda key=key: [
                        (get(name), i, False)
                        for name, order in rows_of(key)
                        for i in range(len(order))
                    ],
                    turn,
                )

        def projection(name, keys):
            values = []
            places = []
            for shift in range(halves):
                away = f"t{shift}" if shift else ""
                for place, key in enumerate(keys):
                    if key == 0:
                        values.append(in_vmem(get(away + "o")) if shift else in_hbm(own))
                        places.append((place, shift, [None] * group))
                        continue
                    if shift:
                        values.append(in_vmem(get(f"{away}k{key}")))
                        places.append((place, shift, sum([js for _, js in rows_of(key)], [])))
                        continue
                    for source, order in rows_of(key):
                        values.append(in_vmem(get(source)))
                        places.append((place, shift, order))
            return project(
                name, pos, cols, counts, potential, values, places, inside, halves
            )

        plan["q"] = (
            lambda: [projection("project", range(group - 1))],
            lambda value: value,
        )
        done["i"] = {
            "cols": block_cols.reshape(-1),
            "counts": block_counts.reshape(-1),
            "pairing": partners.reshape(-1),
            **joins,
        }
        done["i"] = lax.optimization_barrier((done["i"], get("c0")))[0]
        cols, counts, pairing = (done["i"][name] for name in ("cols", "counts", "pairing"))
        for name in WAITS:
            if name in plan:
                get(name)
        projected = get("q")
        projected_last = projection("project_last", [group - 1])
        early = [(part(j)[0], 1) for j in range(group)]
        for key in range(1, 2 * far - 1):
            early += [(get(f"s{key}.{i}"), len(js)) for i, js in enumerate(sizes[key])]
        key = 2 * far - 1
        late = [(get(f"s{key}.{i}"), len(js)) for i, js in enumerate(sizes[key])]
        total = couple(
            "couple",
            False,
            pos,
            pairing,
            [(projected, 0, early, None)],
            group,
            inside,
            outside,
            halves,
        )
        total = couple(
            "couple_last",
            True,
            pos,
            pairing,
            [(projected, 2 * far - 1, late, total), (projected_last, 0, early + late, None)],
            group,
            inside,
            outside,
            halves,
        )
        summed = total[0]
        for shift in range(1, halves):
            summed = summed + rotate(total[shift], shift)
        summed = summed.reshape((group, modes) + summed.shape[1:])
        for i in reversed(range(len(inside))):
            kept = 1 << i
            away = swap(summed[kept:].astype(jnp.bfloat16), 1 << inside[i])
            summed = summed[:kept] + away.astype(jnp.float32)
        result = summed[0]
        return result[:, None] / gaps

    return jax.shard_map(
        per_device,
        mesh=mesh,
        in_specs=(
            P("ka", "orb", None),
            P(None, "orb", None, None, None),
            P(None, "orb", None),
            P(None, "orb"),
            P(),
            P(None, "ka", "orb", None),
        ),
        out_specs=P(None, "ka", "orb", None),
        check_vma=False,
    )
```
